512 devices in a mesh: enc: 16 (over y, core), seq: 32 (over z, x).
Axes of the slice: x: 4, y: 8, z: 8, core: 2. Of those that a mesh axis runs over, the one named last changes fastest.
Arguments:
- clip_features: bfloat16 [16, 32, 4, 16, 16, 512], P('enc', 'seq'), may hold values from -6 to 6
- clip_shape: int32 [16, 32, 3], P('enc', 'seq'), may hold values from 0 to 16, as said below
- packing: int32 [16, 32, 2, 2], P('enc', 'seq'), may hold values from -1 to 15, as said below
- conv_weight: bfloat16 [27, 16, 512], replicated, may hold values from -0.0546875 to 0.0546875
- embed_weight: bfloat16 [64, 2048], replicated, may hold values from -0.75 to 0.75
- mod_shift: float32 [2048], replicated, may hold values from -3 to 3
- mod_scale: float32 [2048], replicated, may hold values from -2 to 2
- qkv_weight: bfloat16 [3, 2048, 2048], P(None, 'seq', 'enc'), may hold values from -0.125 to 0.125
- q_gain: float32 [128], replicated, may hold values from 0.9 to 1.8
- k_gain: float32 [128], replicated, may hold values from 0.9 to 1.8
Outputs:
- attended: bfloat16 [32, 2048, 2048], P('seq', 'enc')
The draws below stay inside these ranges and needn't reach their ends.
Inputs may be any that keep to these rules, and one draw needn't show every extreme that they name: `clip_shape`: Frames, height and width of each device's clip in latent pixels; height and width are even and at least 2, frames at most 4, height at most 16, width at most 16, and frames * height * width / 4 at most 256. Frames is 0 on some devices of every seq index; in every draw some device of each seq index has a clip of 4 x 16 x 16. `packing`: for each block slot: the enc index that owns it in its buffer and its block offset there, below the number of enc devices and below 1; both are -1 exactly for the slots past a clip's last token. Among the devices of one seq index no two blocks name the same owner and offset.
All inputs are finite; a program needn't handle non-finite values.
Results may differ from the reference program's by a relative error of at most 0.0075.
Values may be sent and summed in bfloat16 or wider, within the bound.
A program may use at most 128 MiB of HBM per device.

```python
import jax
import jax.numpy as jnp
from jax import lax

D = 2048
HEADS = 16
HD = 128
LAT = 16
LATF = 64
FEAT = 512
BLOCK = 128
ROWS = 128
FC = 4
HC = 16
WC = 16
NBS = 2
N_ENC = 16
N_SEQ = 32


def pack_plan(key):
    half_hcap = HC // 2
    half_wcap = WC // 2
    own_blocks = ROWS // BLOCK
    slot_count = N_ENC * own_blocks
    spare_slots = slot_count - NBS
    unit_count = (N_ENC - 1) * NBS

    def column(column_key):
        key_take, key_order, key_forced, key_height, key_width, key_slots = jax.random.split(column_key, 6)
        taken_units = spare_slots - jax.random.randint(key_take, (), 0, spare_slots // 4 + 1)
        taken_units = jnp.minimum(taken_units, unit_count)
        unit_order = jax.random.permutation(key_order, unit_count)
        unit_rank = jnp.argsort(unit_order)
        chosen = (unit_rank < taken_units).astype(jnp.int32).reshape(N_ENC - 1, NBS).sum(1)
        forced = jax.random.randint(key_forced, (), 0, N_ENC)
        device_ix = jnp.arange(N_ENC)
        before = chosen[jnp.clip(device_ix, 0, N_ENC - 2)]
        shifted_up = chosen[jnp.clip(device_ix - 1, 0, N_ENC - 2)]
        block_count = jnp.where(device_ix < forced, before, jnp.where(device_ix == forced, NBS, shifted_up))
        need_tokens = (BLOCK * block_count + FC - 1) // FC
        low_h = jnp.maximum(1, (need_tokens + half_wcap - 1) // half_wcap)
        half_h = jax.random.randint(key_height, (N_ENC,), low_h, half_hcap + 1)
        low_w = jnp.maximum(1, (need_tokens + half_h - 1) // half_h)
        half_w = jax.random.randint(key_width, (N_ENC,), low_w, half_wcap + 1)
        frames = BLOCK * block_count // (half_h * half_w)
        dims = jnp.stack([frames, 2 * half_h, 2 * half_w], -1).astype(jnp.int32)
        first_rank = jnp.cumsum(block_count) - block_count
        position = first_rank[:, None] + jnp.arange(NBS)[None, :]
        is_live = jnp.arange(NBS)[None, :] < block_count[:, None]
        rest_order = jax.random.permutation(key_slots, slot_count - 1)
        slot_order = jnp.concatenate([jnp.full((1,), slot_count - 1, jnp.int32), rest_order.astype(jnp.int32)])
        slot_ix = slot_order[jnp.clip(position, 0, slot_count - 1)]
        plan_rows = jnp.stack([jnp.where(is_live, slot_ix // own_blocks, -1), jnp.where(is_live, slot_ix % own_blocks, -1)], -1)
        return (dims, plan_rows.astype(jnp.int32))
    column_keys = jax.random.split(key, N_SEQ)
    shapes, plan_all = jax.vmap(column)(column_keys)
    return (shapes.transpose(1, 0, 2), plan_all.transpose(1, 0, 2, 3))


def draw_clip_shape(key, part):
    shapes, plan_all = pack_plan(key)
    return shapes


def draw_packing(key, part):
    shapes, plan_all = pack_plan(key)
    return plan_all


def block_scale(rng, shape, cuts, smallest, largest):
    def one(dim, shards_of):
        steps = jax.random.uniform(jax.random.fold_in(jax.random.fold_in(rng, 6), dim), (shards_of,), jnp.float32, smallest / len(cuts), largest / len(cuts))
        return jnp.repeat(jnp.exp(steps), shape[dim] // shards_of).reshape((-1,) + (1,) * (len(shape) - dim - 1))

    factor_of = one(*cuts[0])
    for cut in cuts[1:]:
        factor_of = factor_of * one(*cut)
    return factor_of


def centred(key, shape, scale, bound, cuts=(), dtype=jnp.bfloat16):
    drawn = jax.random.normal(key, shape, jnp.float32) * scale
    if len(cuts) > 0:
        drawn = block_scale(key, shape, cuts, -0.22, 0.18) * drawn
    return jnp.clip(drawn, min=-bound, max=bound).astype(dtype)


def setup_inputs(seed: int = 0) -> dict:
    key_of = jax.random.split(jax.random.key(seed), 11)
    return {
        "clip_features": centred(key_of[0], (N_ENC, N_SEQ, FC, HC, WC, FEAT), 1.0, 6.0, ((0, 16), (1, 32))),
        "clip_shape": draw_clip_shape(jax.random.fold_in(key_of[10], 71), 0),
        "packing": draw_packing(jax.random.fold_in(key_of[10], 71), 0),
        "conv_weight": centred(key_of[3], (27, LAT, FEAT), (27 * FEAT) ** -0.5, 0.0546875),
        "embed_weight": centred(key_of[4], (LATF, D), LATF ** -0.5, 0.75),
        "mod_shift": centred(key_of[5], (D,), 0.5, 3.0, (), jnp.float32),
        "mod_scale": centred(key_of[6], (D,), 0.3, 2.0, (), jnp.float32),
        "qkv_weight": centred(key_of[7], (3, D, HEADS * HD), D ** -0.5, 0.125, ((1, 32), (2, 16))),
        "q_gain": jnp.clip(jax.random.uniform(key_of[8], (HD,), jnp.float32, 0.9, 1.8), 0.9, 1.8),
        "k_gain": jnp.clip(jax.random.uniform(key_of[9], (HD,), jnp.float32, 0.9, 1.8), 0.9, 1.8),
    }


eps_norm = 1e-06

def encode(features, clip_dims, conv_weight):
    frames_cap, height_cap, width_cap, feat_count = features.shape
    half_h = height_cap // 2
    half_w = width_cap // 2
    latent_ch = conv_weight.shape[1]
    frame_ix = jnp.arange(frames_cap)[:, None, None]
    row_ix = jnp.arange(height_cap)[None, :, None]
    col_ix = jnp.arange(width_cap)[None, None, :]
    inside = (frame_ix < clip_dims[0]) & (row_ix < clip_dims[1]) & (col_ix < clip_dims[2])
    masked = jnp.where(inside[..., None], features, jnp.zeros_like(features))
    padded = jnp.pad(masked, ((2, 0), (1, 1), (1, 1), (0, 0)))
    summed = jnp.zeros((latent_ch, frames_cap * height_cap * width_cap), jnp.float32)
    for tap_depth in range(3):
        for tap_row in range(3):
            for tap_col in range(3):
                shifted = padded[tap_depth:tap_depth + frames_cap, tap_row:tap_row + height_cap, tap_col:tap_col + width_cap]
                shifted = shifted.reshape(-1, feat_count)
                summed = summed + lax.dot_general(conv_weight[9 * tap_depth + 3 * tap_row + tap_col], shifted, (((1,), (1,)), ((), ())), preferred_element_type=jnp.float32)
    latent_map = summed.astype(jnp.bfloat16).reshape(latent_ch, frames_cap, half_h, 2, half_w, 2)
    patches = latent_map.transpose(0, 3, 5, 1, 2, 4).reshape(4 * latent_ch, frames_cap * half_h * half_w)
    clip_h = clip_dims[1] // 2
    clip_w = clip_dims[2] // 2
    per_frame = clip_h * clip_w
    token_ix = jnp.arange(NBS * BLOCK).astype(jnp.int32)
    frame_of = token_ix // per_frame
    within = token_ix % per_frame
    grid_ix = frame_of * (half_h * half_w) + within // clip_w * half_w + within % clip_w
    is_live = token_ix < clip_dims[0] * per_frame
    grid_ix = jnp.where(is_live, grid_ix, 0).astype(jnp.int32)
    tokens = jnp.where(is_live[None, :], jnp.take(patches, grid_ix, axis=1), jnp.zeros((), jnp.bfloat16))
    blocks = tokens.reshape(4 * latent_ch, NBS, BLOCK).transpose(1, 0, 2)
    counts = jnp.clip(clip_dims[0] * per_frame - jnp.arange(NBS).astype(jnp.int32) * BLOCK, 0, BLOCK).astype(jnp.int32)
    return (blocks, counts)

def qk_norm(projected, scale_gain, head_dim):
    per_head = projected.reshape(projected.shape[0], -1, head_dim)
    normed = per_head * lax.rsqrt(lax.optimization_barrier(jnp.mean(per_head * per_head, -1, keepdims=True)) + eps_norm) * scale_gain
    return normed.astype(jnp.bfloat16).reshape(projected.shape)

def norm_project(embedded, mod_shift, mod_scale, weights, q_gain, k_gain):
    head_dim = q_gain.shape[0]
    widened = embedded.astype(jnp.float32)
    row_mean = lax.optimization_barrier(jnp.mean(widened, -1, keepdims=True))
    centered = widened - row_mean
    row_var = lax.optimization_barrier(jnp.mean(centered * centered, -1, keepdims=True))
    normed_rows = (centered * lax.rsqrt(row_var + eps_norm) * (1.0 + mod_scale) + mod_shift).astype(jnp.bfloat16)
    query_raw = jnp.dot(normed_rows, weights[0], preferred_element_type=jnp.float32)
    key_raw = jnp.dot(normed_rows, weights[1], preferred_element_type=jnp.float32)
    value_raw = jnp.dot(normed_rows, weights[2], preferred_element_type=jnp.float32)
    return (qk_norm(query_raw, q_gain, head_dim), qk_norm(key_raw, k_gain, head_dim), value_raw.astype(jnp.bfloat16))

def reference(clip_features, clip_shape, packing, conv_weight, embed_weight, mod_shift, mod_scale, qkv_weight, q_gain, k_gain):
    head_dim = q_gain.shape[0]
    latf = embed_weight.shape[0]
    device_total = N_ENC * N_SEQ
    feats = clip_features.reshape((device_total,) + clip_features.shape[2:])
    dims_flat = clip_shape.reshape(device_total, 3)
    blocks, counts = lax.map(lambda inputs: encode(inputs[0], inputs[1], conv_weight), (feats, dims_flat))
    blocks = blocks.reshape(N_ENC, N_SEQ, NBS, latf, BLOCK).transpose(1, 0, 2, 3, 4)
    counts = counts.reshape(N_ENC, N_SEQ, NBS).transpose(1, 0, 2)
    plan_all = packing.transpose(1, 0, 2, 3)
    own_blocks = ROWS // BLOCK
    buffer_rows = N_ENC * ROWS

    def column(inputs):
        col_blocks, col_counts, col_plan = inputs
        item_count = N_ENC * NBS
        flat_blocks = col_blocks.reshape(item_count, latf, BLOCK)
        flat_counts = col_counts.reshape(item_count)
        flat_plan = col_plan.reshape(item_count, 2)
        source = (jnp.arange(item_count) // NBS).astype(jnp.int32)
        owner_ix = jnp.arange(N_ENC).astype(jnp.int32)[:, None, None]
        offset_ix = jnp.arange(own_blocks).astype(jnp.int32)[None, :, None]
        selector = (flat_plan[:, 0][None, None, :] == owner_ix) & (flat_plan[:, 1][None, None, :] == offset_ix)
        packed = jnp.einsum('eoj,jfb->eofb', selector.astype(jnp.float32), flat_blocks.astype(jnp.float32)).astype(jnp.bfloat16)
        seg_ids = lax.optimization_barrier(jnp.sum(jnp.where(selector, source[None, None, :] + 1, 0), -1))
        live_rows = lax.optimization_barrier(jnp.sum(jnp.where(selector, flat_counts[None, None, :], 0), -1))
        position = jnp.arange(BLOCK).astype(jnp.int32)[None, None, :]
        seg_rows = jnp.where(position < live_rows[..., None], seg_ids[..., None], 0).reshape(buffer_rows).astype(jnp.int32)
        row_latent = packed.transpose(0, 1, 3, 2).reshape(buffer_rows, latf)
        embedded = jnp.dot(row_latent, embed_weight, preferred_element_type=jnp.float32).astype(jnp.bfloat16)
        query_rows, key_rows, value_rows = norm_project(embedded, mod_shift, mod_scale, qkv_weight, q_gain, k_gain)
        same_seg = seg_rows[:, None] == seg_rows[None, :]

        def one_head(head_parts):
            query_head, key_head, value_head = head_parts
            scores = jnp.dot(query_head, key_head.T, preferred_element_type=jnp.float32) * head_dim ** (-0.5)
            exp_scores = jnp.where(same_seg, jnp.exp(scores), 0.0)
            attn_weights = (exp_scores / lax.optimization_barrier(jnp.sum(exp_scores, -1, keepdims=True))).astype(jnp.bfloat16)
            return jnp.dot(attn_weights, value_head, preferred_element_type=jnp.float32).astype(jnp.bfloat16)

        def split_heads(rows_in):
            return rows_in.reshape(buffer_rows, HEADS, head_dim).transpose(1, 0, 2)
        head_out = lax.map(one_head, (split_heads(query_rows), split_heads(key_rows), split_heads(value_rows)))
        return head_out.transpose(1, 0, 2).reshape(buffer_rows, HEADS * head_dim)
    return lax.map(column, (blocks, counts, plan_all))
```

```python
import functools
import math

import jax
import jax.numpy as jnp
from jax import lax
from jax.experimental import pallas as pl
from jax.experimental.pallas import tpu as pltpu
from jax.sharding import PartitionSpec as P

MESH = pl.DeviceIdType.MESH
F32 = jnp.float32
BF16 = jnp.bfloat16
EPS = 1e-06
LATF = 64
LAT = 16
TOK = 256
BLOCK = 128
FRAME = 256
FC = 4
HD = 128


def mod(a, n):
    return lax.rem(a, n)


def near_first(n):
    order = []
    for d in range(1, n // 2 + 1):
        order.append(d)
        if n - d != d:
            order.append(n - d)
    return order


def split_bf16(value, terms):
    parts = []
    for _ in range(terms):
        part = value.astype(BF16)
        parts.append(part)
        value = value - part.astype(F32)
    return parts


def nt_dot(a, b):
    return lax.dot_general(a, b, (((1,), (1,)), ((), ())), preferred_element_type=F32)


def partial_fold(s, embed_ref, scale_ref, shift_ref, w_ref):
    embed = embed_ref[...].astype(F32)
    mean = jnp.mean(embed, -1, keepdims=True)
    window = pl.ds(pl.multiple_of((s // 2) * 128, 128), 128)
    a_part = (embed_ref[:, window].astype(F32) - mean) * (1.0 + scale_ref[:, window])
    shift_rows = jnp.broadcast_to(shift_ref[:, window], (16, 128))
    lhs = jnp.concatenate([a_part, shift_rows], 0)
    hi, lo = split_bf16(lhs, 2)
    lhs2 = jnp.concatenate([hi, lo], 1)
    half = lax.broadcasted_iota(jnp.int32, (128, 3 * HD), 0) // 64
    w_all = jnp.concatenate([w_ref[0], w_ref[1], w_ref[2]], 1).astype(F32)
    w_two = jnp.concatenate([w_all, w_all], 0)
    w_pad = jnp.where(half == mod(s, 2), w_two, 0.0).astype(BF16)
    rhs = jnp.concatenate([w_pad, w_pad], 0)
    return jnp.dot(lhs2, rhs, preferred_element_type=F32)


def token_places(frames, height, width):
    slot = lax.broadcasted_iota(jnp.int32, (1, TOK), 1).astype(F32)
    zero = jnp.zeros((1, TOK), jnp.int32)
    frames_v = (zero + frames).astype(F32)
    half_h = (zero + height).astype(F32) * 0.5
    half_w = (zero + width).astype(F32) * 0.5
    per_frame = half_h * half_w
    t = jnp.floor((slot + 0.5) / per_frame)
    within = slot - t * per_frame
    r = jnp.floor((within + 0.5) / half_w)
    q = within - r * half_w
    count = frames_v * per_frame
    return jnp.where(slot < count, t * FRAME + r * 32.0 + q * 2.0, -1.0), count


def clip_tokens(frames, height, width, feat_ref, conv_ref):
    lane = lax.broadcasted_iota(jnp.int32, (1, FRAME), 1)
    row, col = lane // 16, lane % 16
    inside = (row < height) & (col < width)
    conv = conv_ref[...]
    places, count = token_places(frames, height, width)
    spot = lax.broadcasted_iota(jnp.int32, (FRAME, TOK), 0).astype(F32)
    products = []
    tokens = jnp.zeros((LATF, TOK), F32)
    taps = 9 * LAT
    for t in range(FC):
        here = nt_dot(conv, feat_ref[t * FRAME : (t + 1) * FRAME, :])
        keep = inside & (lane < jnp.where(t < frames, FRAME, 0))
        products.append(jnp.where(keep, here, 0.0))
        summed = products[t][2 * taps :]
        if t >= 1:
            summed = summed + products[t - 1][taps : 2 * taps]
        if t >= 2:
            summed = summed + products[t - 2][:taps]
        third = 3 * LAT
        rows = summed[third : 2 * third]
        rows = rows + jnp.where(row >= 1, pltpu.roll(summed[:third], 16, 1), 0.0)
        rows = rows + jnp.where(row <= 14, pltpu.roll(summed[2 * third :], FRAME - 16, 1), 0.0)
        latent = rows[LAT : 2 * LAT]
        latent = latent + jnp.where(col >= 1, pltpu.roll(rows[:LAT], 1, 1), 0.0)
        latent = latent + jnp.where(col <= 14, pltpu.roll(rows[2 * LAT :], FRAME - 1, 1), 0.0)
        latent = latent.astype(BF16).astype(F32)
        phases = [latent] + [pltpu.roll(latent, FRAME - d, 1) for d in (1, 16, 17)]
        phases = jnp.concatenate(phases, 0).astype(BF16)
        pick = jnp.where(spot + float(t * FRAME) == places, 1.0, 0.0).astype(BF16)
        tokens = tokens + jnp.dot(phases, pick, preferred_element_type=F32)
    out_row = lax.broadcasted_iota(jnp.int32, (LATF, LATF), 0)
    in_row = lax.broadcasted_iota(jnp.int32, (LATF, LATF), 1)
    swap = jnp.where(in_row == (out_row % 4) * LAT + out_row // 4, 1.0, 0.0).astype(BF16)
    tokens = jnp.dot(swap, tokens.astype(BF16), preferred_element_type=F32)
    return tokens.astype(BF16), count


def gram_terms(embed_ref):
    embed = embed_ref[...]
    features = embed.shape[1]
    both = nt_dot(embed, embed)
    wide = embed.astype(F32)
    mean_col = jnp.mean(wide, -1, keepdims=True)
    ones = jnp.ones((8, features), BF16)
    mean_row = nt_dot(ones, embed)[:1] * (1.0 / features)
    gram = both * (1.0 / features) - mean_col * mean_row
    return jnp.concatenate(split_bf16(gram, 3), 0)


def move_kernel(
    ny,
    nz,
    nx,
    dims_ref,
    plan_ref,
    feat_hbm,
    conv_ref,
    embed_ref,
    scale_ref,
    shift_ref,
    w_ref,
    xt_ref,
    xq_ref,
    rk_ref,
    rq_ref,
    same_ref,
    fold_ref,
    head_ref,
    feat_ref,
    stage,
    sum_in,
    own_sum,
    cross_in,
    x_all,
    feat_sem,
    send1,
    recv1,
    send2,
    recv2,
    send3,
    recv3,
    send4,
    recv4,
    send5,
    recv5,
    send6,
    recv6,
    send7,
    recv7,
):
    e = lax.axis_index("enc")
    s = lax.axis_index("seq")
    y, c = e // 2, mod(e, 2)
    z, x = s // nx, mod(s, nx)
    group = LATF // nz
    rows = 3 * group + 8

    def at_y(d):
        return {"enc": mod(y + d, ny) * 2 + c, "seq": s}

    def at_z(d):
        return {"enc": e, "seq": mod(z + d, nz) * nx + x}

    def at_x(d):
        return {"enc": e, "seq": z * nx + mod(x + d, nx)}

    sibling = {"enc": y * 2 + 1 - c, "seq": s}

    feat_copy = pltpu.make_async_copy(feat_hbm, feat_ref, feat_sem)
    feat_copy.start()

    barrier = pltpu.get_barrier_semaphore()
    peers = [at_z(d) for d in range(1, nz)] + [at_x(d) for d in range(1, nx)]
    peers += [at_y(d) for d in range(1, ny)] + [sibling]
    for peer in peers:
        pl.semaphore_signal(barrier, inc=1, device_id=peer, device_id_type=MESH)

    sends = []

    def send(src, dst, send_sem, recv_sem, peer):
        copy = pltpu.make_async_remote_copy(
            src_ref=src,
            dst_ref=dst,
            send_sem=send_sem,
            recv_sem=recv_sem,
            device_id=peer,
            device_id_type=MESH,
        )
        copy.start()
        sends.append(copy)
        return copy

    part = partial_fold(s, embed_ref, scale_ref, shift_ref, w_ref)
    row8 = lax.broadcasted_iota(jnp.int32, (8, HD), 0)
    bias = jnp.zeros((8, HD), F32)
    for j in range(3):
        bias = jnp.where(row8 == j, part[LATF : LATF + 8, j * HD : (j + 1) * HD], bias)
    for g in range(nz):
        for j in range(3):
            stage[g, j * group : (j + 1) * group, :] = part[
                g * group : (g + 1) * group, j * HD : (j + 1) * HD
            ]
        stage[g, 3 * group :, :] = bias

    pl.semaphore_wait(barrier, len(peers))

    first = [
        send(stage.at[mod(z + d, nz)], sum_in.at[d], send1.at[d], recv1.at[d], at_z(d))
        for d in near_first(nz)
    ]

    feat_copy.wait()
    frames, height, width = dims_ref[0], dims_ref[1], dims_ref[2]
    tokens, count = clip_tokens(frames, height, width, feat_ref, conv_ref)
    for b in range(2):
        for i in range(4):
            x_all[e, 4 * b + i] = tokens[16 * i : 16 * i + 16, b * BLOCK : (b + 1) * BLOCK]
    row16 = lax.broadcasted_iota(jnp.int32, (16, BLOCK), 0)
    owner0 = (jnp.zeros((16, BLOCK), jnp.int32) + plan_ref[0]).astype(F32)
    owner1 = (jnp.zeros((16, BLOCK), jnp.int32) + plan_ref[2]).astype(F32)
    meta = jnp.where(row16 == 0, owner0, jnp.where(row16 == 1, owner1, count[:, :BLOCK]))
    x_all[e, 8] = meta.astype(BF16)
    x_first = [
        send(x_all.at[e], x_all.at[e], send6.at[d], recv6.at[d], at_y(d)) for d in near_first(ny)
    ]
    x_own = send(x_all.at[e], x_all.at[e], send7.at[0], recv7.at[0], sibling)

    total = stage[z]
    for copy in first:
        copy.wait_recv()
    for d in range(1, nz):
        total = total + sum_in[d]
    own_sum[...] = total
    second = [
        send(own_sum, cross_in.at[d], send2.at[d], recv2.at[d], at_x(d)) for d in near_first(nx)
    ]
    gram = gram_terms(embed_ref)
    for copy in second:
        copy.wait_recv()
    for d in range(1, nx):
        total = total + cross_in[d]

    bias = total[3 * group :]
    bias_hi = bias.astype(BF16).astype(F32)
    tail = jnp.where(row8 < 3, bias_hi, pltpu.roll(bias - bias_hi, 3, 0))
    head_ref[c, y] = jnp.concatenate([total[: 3 * group], tail], 0).astype(BF16)
    third = [
        send(head_ref.at[c, y], head_ref.at[c, y], send3.at[d], recv3.at[d], at_y(d))
        for d in near_first(ny)
    ]
    for copy in third:
        copy.wait_recv()

    def pack(core):
        whole = head_ref[core].astype(F32)[:, : 3 * group]
        fold_ref[core, z] = whole.reshape(ny * 3 * group, HD).astype(BF16)

    pack(c)
    fourth = [
        send(fold_ref.at[c, z], fold_ref.at[c, z], send4.at[d], recv4.at[d], at_z(d))
        for d in near_first(nz)
    ]
    fifth = [send(head_ref.at[c], head_ref.at[c], send5.at[0], recv5.at[0], sibling)]

    x_second = [x_own]
    for d, copy in zip(near_first(ny), x_first):
        copy.wait_recv()
        source = mod(y - d + ny, ny) * 2 + c
        x_second.append(
            send(x_all.at[source], x_all.at[source], send7.at[d], recv7.at[d], sibling)
        )
    for copy in x_second:
        copy.wait_recv()

    chosen = jnp.zeros((2, 4, 16, BLOCK), F32)
    is0 = jnp.zeros((1, BLOCK), F32)
    is1 = jnp.zeros((1, BLOCK), F32)
    live = jnp.zeros((1, BLOCK), F32)
    me = (jnp.zeros((1, BLOCK), jnp.int32) + e).astype(F32)
    for j in range(2 * ny):
        info = x_all[j, 8].astype(F32)
        here0 = jnp.where(info[0:1] == me, 1.0, 0.0)
        here1 = jnp.where(info[1:2] == me, 1.0, 0.0)
        here = here0 + here1
        is0, is1 = is0 + here0, is1 + here1
        live = live + here * info[2:3]
        chosen = chosen + x_all[j, 0:8].astype(F32).reshape(2, 4, 16, BLOCK) * here
    chosen = chosen.reshape(2, LATF, BLOCK)
    xt = jnp.concatenate([chosen[0].T, chosen[1].T], 0)
    xt16 = xt.astype(BF16)
    mixed = jnp.dot(
        jnp.concatenate([xt16, xt16, xt16], 1), gram, preferred_element_type=F32
    )
    var = jnp.sum(mixed * xt, -1, keepdims=True)
    rstd = jnp.broadcast_to(lax.rsqrt(jnp.maximum(var, 0.0) + EPS), (TOK, HD))
    xt_ref[...] = xt16
    xq_ref[...] = (chosen[0] * is0 + chosen[1] * is1).T.astype(BF16)
    rk_ref[...] = rstd
    rq_ref[...] = rstd[:BLOCK] * is0 + rstd[BLOCK:] * is1
    q_slot = lax.broadcasted_iota(jnp.int32, (BLOCK, BLOCK), 0).astype(F32) + is1 * BLOCK
    q_live = jnp.where(q_slot < live, 1.0, 0.0)
    for b in range(2):
        k_slot = lax.broadcasted_iota(jnp.int32, (1, BLOCK), 1).astype(F32) + float(b * BLOCK)
        k_live = jnp.where(k_slot < live, 1.0, 0.0)
        same_ref[:, b * BLOCK : (b + 1) * BLOCK] = jnp.where(q_live == k_live, 1.0, 0.0)

    for d, copy in zip(near_first(nz), fourth):
        copy.wait_recv()
        source = mod(z - d + nz, nz)
        fifth.append(
            send(
                fold_ref.at[c, source],
                fold_ref.at[c, source],
                send5.at[d],
                recv5.at[d],
                sibling,
            )
        )
    for copy in fifth:
        copy.wait_recv()
    pack(1 - c)
    for copy in sends:
        copy.wait_send()


def attend_kernel(
    ny, nz, xt_ref, xq_ref, rk_ref, rq_ref, same_ref, fold_ref, head_ref, qg_ref, kg_ref, out_ref
):
    group = LATF // nz
    xt, xq = xt_ref[...], xq_ref[...]
    rk, rq = rk_ref[...], rq_ref[...]
    same = same_ref[...]
    q_gain = qg_ref[...] * (HD ** -0.5 * math.log2(math.e))
    k_gain = kg_ref[...]
    ones = jnp.ones((TOK, HD), BF16)
    for core in range(2):
        for head in range(ny):
            start = head * 3 * group
            fold = fold_ref[core, :, start : start + 3 * group, :].astype(F32)
            fold = [
                fold[:, j * group : (j + 1) * group].reshape(LATF, HD).astype(BF16)
                for j in range(3)
            ]
            tail = head_ref[core, head].astype(F32)[3 * group :]
            bias = tail[0:3] + tail[3:6]
            q = jnp.dot(xq, fold[0], preferred_element_type=F32) * rq + bias[0:1]
            kv = jnp.dot(xt, jnp.concatenate(fold[1:], 1), preferred_element_type=F32)
            k = kv[:, :HD] * rk + bias[1:2]
            v = (kv[:, HD:] * rk + bias[2:3]).astype(BF16)
            q = q * lax.rsqrt(jnp.mean(q * q, -1, keepdims=True) + EPS) * q_gain
            k = k * lax.rsqrt(jnp.mean(k * k, -1, keepdims=True) + EPS) * k_gain
            scores = nt_dot(q.astype(BF16), k.astype(BF16))
            weights = (jnp.exp2(scores) * same).astype(BF16)
            mixed = jnp.dot(weights, jnp.concatenate([v, ones], 1), preferred_element_type=F32)
            column = (2 * head + core) * HD
            out_ref[:, column : column + HD] = (mixed[:, :HD] / mixed[:, HD:]).astype(BF16)


def whole(memory=pltpu.VMEM):
    return pl.BlockSpec(memory_space=memory)


def solution(mesh):
    ny = mesh.shape["enc"] // 2
    nx = 4 if mesh.shape["seq"] == 32 else 2
    nz = mesh.shape["seq"] // nx
    group = LATF // nz
    rows = 3 * group + 8
    dma = pltpu.SemaphoreType.DMA

    def on_device(
        clip_features,
        clip_shape,
        packing,
        conv_weight,
        embed_weight,
        mod_shift,
        mod_scale,
        qkv_weight,
        q_gain,
        k_gain,
    ):
        features = clip_features.shape[-1]
        moved = pl.pallas_call(
            functools.partial(move_kernel, ny, nz, nx),
            out_shape=(
                jax.ShapeDtypeStruct((TOK, LATF), BF16),
                jax.ShapeDtypeStruct((BLOCK, LATF), BF16),
                jax.ShapeDtypeStruct((TOK, HD), F32),
                jax.ShapeDtypeStruct((BLOCK, HD), F32),
                jax.ShapeDtypeStruct((BLOCK, TOK), F32),
                jax.ShapeDtypeStruct((2, nz, ny * 3 * group, HD), BF16),
                jax.ShapeDtypeStruct((2, ny, rows, HD), BF16),
            ),
            in_specs=[
                whole(pltpu.SMEM),
                whole(pltpu.SMEM),
                whole(pl.ANY),
                whole(),
                whole(),
                whole(),
                whole(),
                whole(),
            ],
            out_specs=tuple(whole() for _ in range(7)),
            scratch_shapes=[
                pltpu.VMEM((FC * FRAME, features), BF16),
                pltpu.VMEM((nz, rows, HD), F32),
                pltpu.VMEM((nz, rows, HD), F32),
                pltpu.VMEM((rows, HD), F32),
                pltpu.VMEM((nx, rows, HD), F32),
                pltpu.VMEM((2 * ny, 9, 16, BLOCK), BF16),
                dma(()),
                dma((nz,)),
                dma((nz,)),
                dma((nx,)),
                dma((nx,)),
                dma((ny,)),
                dma((ny,)),
                dma((nz,)),
                dma((nz,)),
                dma((nz,)),
                dma((nz,)),
                dma((ny,)),
                dma((ny,)),
                dma((ny,)),
                dma((ny,)),
            ],
            compiler_params=pltpu.CompilerParams(
                collective_id=0, has_side_effects=True, vmem_limit_bytes=40 * 1024 * 1024
            ),
            name="encode_and_move",
        )(
            clip_shape.reshape(3),
            packing.reshape(4),
            clip_features.reshape(FC * FRAME, features),
            conv_weight.reshape(-1, features),
            embed_weight,
            mod_scale.reshape(1, -1),
            mod_shift.reshape(1, -1),
            qkv_weight,
        )
        out = pl.pallas_call(
            functools.partial(attend_kernel, ny, nz),
            out_shape=jax.ShapeDtypeStruct((BLOCK, 2 * ny * HD), BF16),
            in_specs=[whole() for _ in range(9)],
            out_specs=whole(),
            compiler_params=pltpu.CompilerParams(vmem_limit_bytes=40 * 1024 * 1024),
            name="attend",
        )(*moved, q_gain.reshape(1, -1), k_gain.reshape(1, -1))
        return out[None]

    return jax.shard_map(
        on_device,
        mesh=mesh,
        in_specs=(
            P("enc", "seq", None, None, None, None),
            P("enc", "seq", None),
            P("enc", "seq", None, None),
            P(),
            P(),
            P(),
            P(),
            P(None, "seq", "enc"),
            P(),
            P(),
        ),
        out_specs=P("seq", "enc", None),
        check_vma=False,
    )
```

```python
import functools
import math

import jax
import jax.numpy as jnp
from jax import lax
from jax.experimental import pallas as pl
from jax.experimental.pallas import tpu as pltpu
from jax.sharding import PartitionSpec as P

MESH = pl.DeviceIdType.MESH
F32 = jnp.float32
BF16 = jnp.bfloat16
EPS = 1e-06
LATF = 64
LAT = 16
TOK = 256
BLOCK = 128
FRAME = 256
FC = 4
HD = 128


def mod(a, n):
    return lax.rem(a, n)


def near_first(n):
    order = []
    for d in range(1, n // 2 + 1):
        order.append(d)
        if n - d != d:
            order.append(n - d)
    return order


def split_bf16(value, terms):
    parts = []
    for _ in range(terms):
        part = value.astype(BF16)
        parts.append(part)
        value = value - part.astype(F32)
    return parts


def nt_dot(a, b):
    return lax.dot_general(a, b, (((1,), (1,)), ((), ())), preferred_element_type=F32)


def partial_fold(s, embed_ref, scale_ref, shift_ref, w_ref):
    embed = embed_ref[...].astype(F32)
    mean = jnp.mean(embed, -1, keepdims=True)
    window = pl.ds(pl.multiple_of((s // 2) * 128, 128), 128)
    a_part = (embed_ref[:, window].astype(F32) - mean) * (1.0 + scale_ref[:, window])
    shift_rows = jnp.broadcast_to(shift_ref[:, window], (16, 128))
    lhs = jnp.concatenate([a_part, shift_rows], 0)
    hi, lo = split_bf16(lhs, 2)
    lhs2 = jnp.concatenate([hi, lo], 1)
    half = lax.broadcasted_iota(jnp.int32, (128, 3 * HD), 0) // 64
    w_all = jnp.concatenate([w_ref[0], w_ref[1], w_ref[2]], 1).astype(F32)
    w_two = jnp.concatenate([w_all, w_all], 0)
    w_pad = jnp.where(half == mod(s, 2), w_two, 0.0).astype(BF16)
    rhs = jnp.concatenate([w_pad, w_pad], 0)
    return jnp.dot(lhs2, rhs, preferred_element_type=F32)


def token_places(frames, height, width):
    slot = lax.broadcasted_iota(jnp.int32, (1, TOK), 1).astype(F32)
    zero = jnp.zeros((1, TOK), jnp.int32)
    frames_v = (zero + frames).astype(F32)
    half_h = (zero + height).astype(F32) * 0.5
    half_w = (zero + width).astype(F32) * 0.5
    per_frame = half_h * half_w
    t = jnp.floor((slot + 0.5) / per_frame)
    within = slot - t * per_frame
    r = jnp.floor((within + 0.5) / half_w)
    q = within - r * half_w
    count = frames_v * per_frame
    return jnp.where(slot < count, t * FRAME + r * 32.0 + q * 2.0, -1.0), count


def clip_tokens(frames, height, width, feat_ref, conv_ref):
    lane = lax.broadcasted_iota(jnp.int32, (1, FRAME), 1)
    row, col = lane // 16, lane % 16
    inside = (row < height) & (col < width)
    conv = conv_ref[...]
    places, count = token_places(frames, height, width)
    spot = lax.broadcasted_iota(jnp.int32, (FRAME, TOK), 0).astype(F32)
    products = []
    tokens = jnp.zeros((LATF, TOK), F32)
    taps = 9 * LAT
    for t in range(FC):
        here = nt_dot(conv, feat_ref[t * FRAME : (t + 1) * FRAME, :])
        keep = inside & (lane < jnp.where(t < frames, FRAME, 0))
        products.append(jnp.where(keep, here, 0.0))
        summed = products[t][2 * taps :]
        if t >= 1:
            summed = summed + products[t - 1][taps : 2 * taps]
        if t >= 2:
            summed = summed + products[t - 2][:taps]
        third = 3 * LAT
        rows = summed[third : 2 * third]
        rows = rows + jnp.where(row >= 1, pltpu.roll(summed[:third], 16, 1), 0.0)
        rows = rows + jnp.where(row <= 14, pltpu.roll(summed[2 * third :], FRAME - 16, 1), 0.0)
        latent = rows[LAT : 2 * LAT]
        latent = latent + jnp.where(col >= 1, pltpu.roll(rows[:LAT], 1, 1), 0.0)
        latent = latent + jnp.where(col <= 14, pltpu.roll(rows[2 * LAT :], FRAME - 1, 1), 0.0)
        latent = latent.astype(BF16).astype(F32)
        phases = [latent] + [pltpu.roll(latent, FRAME - d, 1) for d in (1, 16, 17)]
        phases = jnp.concatenate(phases, 0).astype(BF16)
        pick = jnp.where(spot + float(t * FRAME) == places, 1.0, 0.0).astype(BF16)
        tokens = tokens + jnp.dot(phases, pick, preferred_element_type=F32)
    out_row = lax.broadcasted_iota(jnp.int32, (LATF, LATF), 0)
    in_row = lax.broadcasted_iota(jnp.int32, (LATF, LATF), 1)
    swap = jnp.where(in_row == (out_row % 4) * LAT + out_row // 4, 1.0, 0.0).astype(BF16)
    tokens = jnp.dot(swap, tokens.astype(BF16), preferred_element_type=F32)
    return tokens.astype(BF16), count


def gram_terms(embed_ref):
    embed = embed_ref[...]
    features = embed.shape[1]
    both = nt_dot(embed, embed)
    wide = embed.astype(F32)
    mean_col = jnp.mean(wide, -1, keepdims=True)
    ones = jnp.ones((8, features), BF16)
    mean_row = nt_dot(ones, embed)[:1] * (1.0 / features)
    gram = both * (1.0 / features) - mean_col * mean_row
    return jnp.concatenate(split_bf16(gram, 3), 0)


def resplit(tile):
    row = lax.broadcasted_iota(jnp.int32, tile.shape, 0)
    total = tile + pltpu.roll(tile, tile.shape[0] - 3, 0)
    high = total.astype(BF16).astype(F32)
    low = pltpu.roll(total - high, 3, 0)
    return jnp.where(row < 3, high, jnp.where(row < 6, low, 0.0))


def pick_clip(e, count, x_all, gram):
    chosen = jnp.zeros((2, 4, 16, BLOCK), F32)
    is1 = jnp.zeros((1, BLOCK), F32)
    live = jnp.zeros((1, BLOCK), F32)
    me = (jnp.zeros((1, BLOCK), jnp.int32) + e).astype(F32)
    for j in range(count):
        info = x_all[j, 8].astype(F32)
        here1 = jnp.where(info[1:2] == me, 1.0, 0.0)
        here = jnp.where(info[0:1] == me, 1.0, 0.0) + here1
        is1 = is1 + here1
        live = live + here * info[2:3]
        chosen = chosen + x_all[j, 0:8].astype(F32).reshape(2, 4, 16, BLOCK) * here
    chosen = chosen.reshape(2, LATF, BLOCK)
    xt = jnp.concatenate([chosen[0].T, chosen[1].T], 0)
    xt16 = xt.astype(BF16)
    mixed = jnp.dot(jnp.concatenate([xt16, xt16, xt16], 1), gram, preferred_element_type=F32)
    var = jnp.sum(mixed * xt, -1, keepdims=True)
    scaled = xt * lax.rsqrt(jnp.maximum(var, 0.0) + EPS)
    high, low = split_bf16(scaled, 2)
    keys = jnp.concatenate([high, low], 1)
    rows = jnp.where(is1 > 0.5, keys[BLOCK:].astype(F32), keys[:BLOCK].astype(F32)).astype(BF16)
    keys = jnp.concatenate([keys, jnp.ones((TOK, 16), BF16)], 1)
    rows = jnp.concatenate([rows, jnp.ones((BLOCK, 16), BF16)], 1)
    q_slot = lax.broadcasted_iota(jnp.int32, (BLOCK, BLOCK), 0).astype(F32) + is1 * BLOCK
    q_live = jnp.where(q_slot < live, 1.0, 0.0)
    same = []
    for b in range(2):
        k_slot = lax.broadcasted_iota(jnp.int32, (1, BLOCK), 1).astype(F32) + float(b * BLOCK)
        k_live = jnp.where(k_slot < live, 1.0, 0.0)
        same.append(jnp.where(q_live == k_live, 1.0, 0.0))
    return keys, rows, jnp.concatenate(same, 1)


def attend_head(keys, rows, same, fold, tail, gain):
    row = lax.broadcasted_iota(jnp.int32, (16, HD), 0)
    tail = tail.astype(F32)
    bias = [jnp.where((row == j) | (row == j + 3), tail, 0.0).astype(BF16) for j in range(3)]
    q = jnp.dot(rows, jnp.concatenate([fold[0], fold[0], bias[0]], 0), preferred_element_type=F32)
    kv_fold = jnp.concatenate(fold[1:], 1)
    kv_bias = jnp.concatenate(bias[1:], 1)
    kv = jnp.dot(
        keys, jnp.concatenate([kv_fold, kv_fold, kv_bias], 0), preferred_element_type=F32
    )
    k = kv[:, :HD]
    v = kv[:, HD:].astype(BF16)
    q = q * (lax.rsqrt(jnp.mean(q * q, -1, keepdims=True) + EPS)) * gain
    k = k * lax.rsqrt(jnp.mean(k * k, -1, keepdims=True) + EPS)
    scores = nt_dot(q.astype(BF16), k.astype(BF16))
    weights = (jnp.exp2(scores) * same).astype(BF16)
    ones = jnp.ones((TOK, HD), BF16)
    mixed = jnp.dot(weights, jnp.concatenate([v, ones], 1), preferred_element_type=F32)
    return (mixed[:, :HD] / mixed[:, HD:]).astype(BF16)


def whole_kernel(
    ny,
    nz,
    nx,
    dims_ref,
    plan_ref,
    feat_hbm,
    conv_hbm,
    embed_hbm,
    scale_hbm,
    shift_hbm,
    w_hbm,
    qg_hbm,
    kg_hbm,
    out_ref,
    feat_ref,
    conv_ref,
    embed_ref,
    scale_ref,
    shift_ref,
    w_ref,
    qg_ref,
    kg_ref,
    stage,
    x_in,
    z_own,
    z_in,
    folds,
    x_all,
    in_sem,
    sendx,
    recvx,
    sendz,
    recvz,
    sendy,
    recvy,
    sendq,
    recvq,
    sendc,
    recvc,
    sendt,
    recvt,
    sendu,
    recvu,
):
    e = lax.axis_index("enc")
    s = lax.axis_index("seq")
    y, c = e // 2, mod(e, 2)
    z, x = s // nx, mod(s, nx)
    part_rows = LATF // nx
    fold_rows = 3 * part_rows

    def at_y(d):
        return {"enc": mod(y + d, ny) * 2 + c, "seq": s}

    def at_z(d):
        return {"enc": e, "seq": mod(z + d, nz) * nx + x}

    def at_x(d):
        return {"enc": e, "seq": z * nx + mod(x + d, nx)}

    sibling = {"enc": y * 2 + 1 - c, "seq": s}

    barrier = pltpu.get_barrier_semaphore()
    peers = [at_z(d) for d in reversed(near_first(nz))] + [at_y(d) for d in reversed(near_first(ny))]
    peers += [at_x(d) for d in reversed(near_first(nx))] + [sibling]
    for peer in peers:
        pl.semaphore_signal(barrier, inc=1, device_id=peer, device_id_type=MESH)

    loads = {}
    for i, (name, src, dst) in enumerate(
        [
            ("embed", embed_hbm, embed_ref),
            ("w", w_hbm, w_ref),
            ("scale", scale_hbm, scale_ref),
            ("shift", shift_hbm, shift_ref),
            ("conv", conv_hbm, conv_ref),
            ("feat", feat_hbm, feat_ref),
            ("qg", qg_hbm, qg_ref),
            ("kg", kg_hbm, kg_ref),
        ]
    ):
        loads[name] = pltpu.make_async_copy(src, dst, in_sem.at[i])
        loads[name].start()

    sends = []

    def send(src, dst, send_sem, recv_sem, peer):
        copy = pltpu.make_async_remote_copy(
            src_ref=src,
            dst_ref=dst,
            send_sem=send_sem,
            recv_sem=recv_sem,
            device_id=peer,
            device_id_type=MESH,
        )
        copy.start()
        sends.append(copy)
        return copy

    for name in ("embed", "w", "scale", "shift"):
        loads[name].wait()
    part = partial_fold(s, embed_ref, scale_ref, shift_ref, w_ref)
    row16 = lax.broadcasted_iota(jnp.int32, (16, HD), 0)
    bias = jnp.zeros((16, HD), F32)
    for j in range(3):
        bias = jnp.where(row16 == j, part[LATF : LATF + 16, j * HD : (j + 1) * HD], bias)
    bias = resplit(bias).astype(BF16)
    for g in range(nx):
        for j in range(3):
            stage[g, j * part_rows : (j + 1) * part_rows, :] = part[
                g * part_rows : (g + 1) * part_rows, j * HD : (j + 1) * HD
            ].astype(BF16)
        stage[g, fold_rows:, :] = bias

    pl.semaphore_wait(barrier, len(peers))

    over_x = [
        send(stage.at[mod(x + d, nx)], x_in.at[d], sendx.at[d], recvx.at[d], at_x(d))
        for d in near_first(nx)
    ]

    for name in ("conv", "feat"):
        loads[name].wait()
    frames, height, width = dims_ref[0, 0, 0], dims_ref[0, 0, 1], dims_ref[0, 0, 2]
    tokens, count = clip_tokens(frames, height, width, feat_ref, conv_ref)
    for b in range(2):
        for i in range(4):
            x_all[e, 4 * b + i] = tokens[16 * i : 16 * i + 16, b * BLOCK : (b + 1) * BLOCK]
    owner0 = (jnp.zeros((16, BLOCK), jnp.int32) + plan_ref[0, 0, 0, 0]).astype(F32)
    owner1 = (jnp.zeros((16, BLOCK), jnp.int32) + plan_ref[0, 0, 1, 0]).astype(F32)
    meta = jnp.where(row16 == 0, owner0, jnp.where(row16 == 1, owner1, count[:, :BLOCK]))
    x_all[e, 8] = meta.astype(BF16)
    x_first = [
        send(x_all.at[e], x_all.at[e], sendt.at[d], recvt.at[d], at_y(d)) for d in near_first(ny)
    ]
    x_second = [send(x_all.at[e], x_all.at[e], sendu.at[0], recvu.at[0], sibling)]

    def finish(total):
        return jnp.concatenate([total[:fold_rows], resplit(total[fold_rows:])], 0).astype(BF16)

    total = stage[x].astype(F32)
    for copy in over_x:
        copy.wait_recv()
    for d in range(1, nx):
        total = total + x_in[d].astype(F32)
    z_own[...] = finish(total)
    over_z = [
        send(z_own, z_in.at[d], sendz.at[d], recvz.at[d], at_z(d))
        for d in reversed(near_first(nz))
    ]
    gram = gram_terms(embed_ref)

    def pass_tokens(d, copy):
        copy.wait_recv()
        source = mod(y - d + ny, ny) * 2 + c
        x_second.append(
            send(x_all.at[source], x_all.at[source], sendu.at[d], recvu.at[d], sibling)
        )

    arriving = list(zip(near_first(ny), x_first))
    early = len(arriving) // 2
    for d, copy in arriving[:early]:
        pass_tokens(d, copy)
    total = z_own[...].astype(F32)
    for copy in over_z:
        copy.wait_recv()
    for d in range(1, nz):
        total = total + z_in[d].astype(F32)
    folds[c, y, x] = finish(total)

    over_y = {}
    for d in near_first(ny):
        mine = folds.at[c, y, x]
        over_y[d] = send(mine, mine, sendy.at[d], recvy.at[d], at_y(d))
    quarters = {}
    crossed = {}

    def source_y(d):
        return mod(y - d + ny, ny)

    def spread(d):
        if d:
            over_y[d].wait_recv()
        piece = folds.at[c, source_y(d), x, pl.ds(0, fold_rows)]
        quarters[d] = [
            send(piece, piece, sendq.at[d, dx], recvq.at[d, dx], at_x(dx))
            for dx in near_first(nx)
        ]

    def cross(d):
        for copy in quarters[d]:
            copy.wait_recv()
        piece = folds.at[c, source_y(d)]
        crossed[d] = send(piece, piece, sendc.at[d], recvc.at[d], sibling)

    spread(0)
    for d, copy in arriving[early:]:
        pass_tokens(d, copy)
    for copy in x_second:
        copy.wait_recv()
    keys, rows, same = pick_clip(e, 2 * ny, x_all, gram)
    for name in ("qg", "kg"):
        loads[name].wait()
    gain = qg_ref[...] * kg_ref[...] * (HD**-0.5 * math.log2(math.e))

    def attend(d, core):
        source = source_y(d)
        fold = [
            folds[core, source, :, j * part_rows : (j + 1) * part_rows, :].reshape(LATF, HD)
            for j in range(3)
        ]
        tail = folds[core, source, x, fold_rows:, :]
        column = pl.ds(pl.multiple_of((2 * source + core) * HD, HD), HD)
        out_ref[:, column] = attend_head(keys, rows, same, fold, tail, gain)

    order = [0] + near_first(ny)
    ahead = 3
    for i in range(1, min(ahead, ny)):
        spread(order[i])
    for i in range(ny):
        if i + ahead < ny:
            spread(order[i + ahead])
        elif i + ahead == ny:
            pass
        cross(order[i]) if order[i] in quarters else None
        attend(order[i], c)
        if i >= 1:
            crossed[order[i - 1]].wait_recv()
            attend(order[i - 1], 1 - c)
    crossed[order[ny - 1]].wait_recv()
    attend(order[ny - 1], 1 - c)
    for copy in sends:
        copy.wait_send()


def whole(memory=pltpu.VMEM):
    return pl.BlockSpec(memory_space=memory)


def solution(mesh):
    ny = mesh.shape["enc"] // 2
    nx = 4 if mesh.shape["seq"] == 32 else 2
    nz = mesh.shape["seq"] // nx
    fold_rows = 3 * LATF // nx
    rows = fold_rows + 16
    dma = pltpu.SemaphoreType.DMA

    def on_device(
        clip_features,
        clip_shape,
        packing,
        conv_weight,
        embed_weight,
        mod_shift,
        mod_scale,
        qkv_weight,
        q_gain,
        k_gain,
    ):
        features = clip_features.shape[-1]
        width = embed_weight.shape[1]
        out = pl.pallas_call(
            functools.partial(whole_kernel, ny, nz, nx),
            out_shape=jax.ShapeDtypeStruct((BLOCK, 2 * ny * HD), BF16),
            in_specs=[whole(pltpu.SMEM)] * 2 + [whole(pl.ANY)] * 8,
            out_specs=whole(),
            scratch_shapes=[
                pltpu.VMEM((FC * FRAME, features), BF16),
                pltpu.VMEM((27 * LAT, features), BF16),
                pltpu.VMEM((LATF, width), BF16),
                pltpu.VMEM((1, width), F32),
                pltpu.VMEM((1, width), F32),
                pltpu.VMEM(qkv_weight.shape, BF16),
                pltpu.VMEM((1, HD), F32),
                pltpu.VMEM((1, HD), F32),
                pltpu.VMEM((nx, rows, HD), BF16),
                pltpu.VMEM((nx, rows, HD), BF16),
                pltpu.VMEM((rows, HD), BF16),
                pltpu.VMEM((nz, rows, HD), BF16),
                pltpu.VMEM((2, ny, nx, rows, HD), BF16),
                pltpu.VMEM((2 * ny, 9, 16, BLOCK), BF16),
                dma((8,)),
                dma((nx,)),
                dma((nx,)),
                dma((nz,)),
                dma((nz,)),
                dma((ny,)),
                dma((ny,)),
                dma((ny, nx)),
                dma((ny, nx)),
                dma((ny,)),
                dma((ny,)),
                dma((ny,)),
                dma((ny,)),
                dma((ny,)),
                dma((ny,)),
            ],
            compiler_params=pltpu.CompilerParams(
                collective_id=0, has_side_effects=True, vmem_limit_bytes=60 * 1024 * 1024
            ),
            name="encode_move_attend",
        )(
            clip_shape,
            packing,
            clip_features.reshape(FC * FRAME, features),
            conv_weight.reshape(-1, features),
            embed_weight,
            mod_scale.reshape(1, -1),
            mod_shift.reshape(1, -1),
            qkv_weight,
            q_gain.reshape(1, -1),
            k_gain.reshape(1, -1),
        )
        return out[None]

    return jax.shard_map(
        on_device,
        mesh=mesh,
        in_specs=(
            P("enc", "seq", None, None, None, None),
            P("enc", "seq", None),
            P("enc", "seq", None, None),
            P(),
            P(),
            P(),
            P(),
            P(None, "seq", "enc"),
            P(),
            P(),
        ),
        out_specs=P("seq", "enc", None),
        check_vma=False,
    )
```

```python
import functools
import math

import jax
import jax.numpy as jnp
from jax import lax
from jax.experimental import pallas as pl
from jax.experimental.pallas import tpu as pltpu
from jax.sharding import PartitionSpec as P

MESH = pl.DeviceIdType.MESH
F32 = jnp.float32
BF16 = jnp.bfloat16
EPS = 1e-06
LATF = 64
LAT = 16
TOK = 256
BLOCK = 128
FRAME = 256
FC = 4
HD = 128


def mod(a, n):
    return lax.rem(a, n)


def near_first(n):
    order = []
    for d in range(1, n // 2 + 1):
        order.append(d)
        if n - d != d:
            order.append(n - d)
    return order


def split_bf16(value, terms):
    parts = []
    for _ in range(terms):
        part = value.astype(BF16)
        parts.append(part)
        value = value - part.astype(F32)
    return parts


def nt_dot(a, b):
    return lax.dot_general(a, b, (((1,), (1,)), ((), ())), preferred_element_type=F32)


def partial_fold(s, embed_ref, scale_ref, shift_ref, w_ref):
    embed = embed_ref[...].astype(F32)
    mean = jnp.mean(embed, -1, keepdims=True)
    window = pl.ds(pl.multiple_of((s // 2) * 128, 128), 128)
    a_part = (embed_ref[:, window].astype(F32) - mean) * (1.0 + scale_ref[:, window])
    shift_rows = jnp.broadcast_to(shift_ref[:, window], (16, 128))
    lhs = jnp.concatenate([a_part, shift_rows], 0)
    hi, lo = split_bf16(lhs, 2)
    lhs2 = jnp.concatenate([hi, lo], 1)
    half = lax.broadcasted_iota(jnp.int32, (128, 3 * HD), 0) // 64
    w_all = jnp.concatenate([w_ref[0], w_ref[1], w_ref[2]], 1).astype(F32)
    w_two = jnp.concatenate([w_all, w_all], 0)
    w_pad = jnp.where(half == mod(s, 2), w_two, 0.0).astype(BF16)
    rhs = jnp.concatenate([w_pad, w_pad], 0)
    return jnp.dot(lhs2, rhs, preferred_element_type=F32)


def token_places(frames, height, width):
    slot = lax.broadcasted_iota(jnp.int32, (1, TOK), 1).astype(F32)
    zero = jnp.zeros((1, TOK), jnp.int32)
    frames_v = (zero + frames).astype(F32)
    half_h = (zero + height).astype(F32) * 0.5
    half_w = (zero + width).astype(F32) * 0.5
    per_frame = half_h * half_w
    t = jnp.floor((slot + 0.5) / per_frame)
    within = slot - t * per_frame
    r = jnp.floor((within + 0.5) / half_w)
    q = within - r * half_w
    count = frames_v * per_frame
    return jnp.where(slot < count, t * FRAME + r * 32.0 + q * 2.0, -1.0), count


def clip_frames(first, last, state, frames, height, width, feat_ref, conv_ref):
    products, tokens = state
    lane = lax.broadcasted_iota(jnp.int32, (1, FRAME), 1)
    row, col = lane // 16, lane % 16
    inside = (row < height) & (col < width)
    conv = conv_ref[...]
    places, _ = token_places(frames, height, width)
    spot = lax.broadcasted_iota(jnp.int32, (FRAME, TOK), 0).astype(F32)
    taps = 9 * LAT
    for t in range(first, last):
        here = nt_dot(conv, feat_ref[t * FRAME : (t + 1) * FRAME, :])
        keep = inside & (lane < jnp.where(t < frames, FRAME, 0))
        products.append(jnp.where(keep, here, 0.0))
        summed = products[t][2 * taps :]
        if t >= 1:
            summed = summed + products[t - 1][taps : 2 * taps]
        if t >= 2:
            summed = summed + products[t - 2][:taps]
        third = 3 * LAT
        rows = summed[third : 2 * third]
        rows = rows + jnp.where(row >= 1, pltpu.roll(summed[:third], 16, 1), 0.0)
        rows = rows + jnp.where(row <= 14, pltpu.roll(summed[2 * third :], FRAME - 16, 1), 0.0)
        latent = rows[LAT : 2 * LAT]
        latent = latent + jnp.where(col >= 1, pltpu.roll(rows[:LAT], 1, 1), 0.0)
        latent = latent + jnp.where(col <= 14, pltpu.roll(rows[2 * LAT :], FRAME - 1, 1), 0.0)
        latent = latent.astype(BF16).astype(F32)
        phases = [latent] + [pltpu.roll(latent, FRAME - d, 1) for d in (1, 16, 17)]
        phases = jnp.concatenate(phases, 0).astype(BF16)
        pick = jnp.where(spot + float(t * FRAME) == places, 1.0, 0.0).astype(BF16)
        tokens = tokens + jnp.dot(phases, pick, preferred_element_type=F32)
    return products, tokens


def in_feature_order(tokens):
    out_row = lax.broadcasted_iota(jnp.int32, (LATF, LATF), 0)
    in_row = lax.broadcasted_iota(jnp.int32, (LATF, LATF), 1)
    swap = jnp.where(in_row == (out_row % 4) * LAT + out_row // 4, 1.0, 0.0).astype(BF16)
    return jnp.dot(swap, tokens.astype(BF16), preferred_element_type=F32).astype(BF16)


def gram_terms(embed_ref):
    embed = embed_ref[...]
    features = embed.shape[1]
    both = nt_dot(embed, embed)
    wide = embed.astype(F32)
    mean_col = jnp.mean(wide, -1, keepdims=True)
    ones = jnp.ones((8, features), BF16)
    mean_row = nt_dot(ones, embed)[:1] * (1.0 / features)
    gram = both * (1.0 / features) - mean_col * mean_row
    return jnp.concatenate(split_bf16(gram, 3), 0)


def resplit(tile):
    row = lax.broadcasted_iota(jnp.int32, tile.shape, 0)
    total = tile + pltpu.roll(tile, tile.shape[0] - 3, 0)
    high = total.astype(BF16).astype(F32)
    low = pltpu.roll(total - high, 3, 0)
    return jnp.where(row < 3, high, jnp.where(row < 6, low, 0.0))


def pick_clip(e, count, x_all, gram):
    chosen = jnp.zeros((2, 4, 16, BLOCK), F32)
    is1 = jnp.zeros((1, BLOCK), F32)
    live = jnp.zeros((1, BLOCK), F32)
    me = (jnp.zeros((1, BLOCK), jnp.int32) + e).astype(F32)
    for j in range(count):
        info = x_all[j, 8].astype(F32)
        here1 = jnp.where(info[1:2] == me, 1.0, 0.0)
        here = jnp.where(info[0:1] == me, 1.0, 0.0) + here1
        is1 = is1 + here1
        live = live + here * info[2:3]
        chosen = chosen + x_all[j, 0:8].astype(F32).reshape(2, 4, 16, BLOCK) * here
    chosen = chosen.reshape(2, LATF, BLOCK)
    xt = jnp.concatenate([chosen[0].T, chosen[1].T], 0)
    xt16 = xt.astype(BF16)
    mixed = jnp.dot(jnp.concatenate([xt16, xt16, xt16], 1), gram, preferred_element_type=F32)
    var = jnp.sum(mixed * xt, -1, keepdims=True)
    scaled = xt * lax.rsqrt(jnp.maximum(var, 0.0) + EPS)
    high, low = split_bf16(scaled, 2)
    keys = jnp.concatenate([high, low], 1)
    rows = jnp.where(is1 > 0.5, keys[BLOCK:].astype(F32), keys[:BLOCK].astype(F32)).astype(BF16)
    q_slot = lax.broadcasted_iota(jnp.int32, (BLOCK, BLOCK), 0).astype(F32) + is1 * BLOCK
    q_live = jnp.where(q_slot < live, 1.0, 0.0)
    same = []
    for b in range(2):
        k_slot = lax.broadcasted_iota(jnp.int32, (1, BLOCK), 1).astype(F32) + float(b * BLOCK)
        k_live = jnp.where(k_slot < live, 1.0, 0.0)
        same.append(jnp.where(q_live == k_live, 1.0, 0.0))
    return keys, rows, jnp.concatenate(same, 1)


def project_head(keys, rows, fold, tail, gain):
    tail = tail.astype(F32)
    bias = tail[0:3] + tail[3:6]
    q_fold = jnp.concatenate([fold[0], fold[0]], 0)
    kv_fold = jnp.concatenate(fold[1:], 1)
    q = jnp.dot(rows, q_fold, preferred_element_type=F32) + bias[0:1]
    kv = jnp.dot(keys, jnp.concatenate([kv_fold, kv_fold], 0), preferred_element_type=F32)
    k = kv[:, :HD] + bias[1:2]
    q = q * lax.rsqrt(jnp.mean(q * q, -1, keepdims=True) + EPS) * gain
    k = k * lax.rsqrt(jnp.mean(k * k, -1, keepdims=True) + EPS)
    return q.astype(BF16), k.astype(BF16), kv[:, HD:].astype(BF16), bias[2:3]


def mix_head(q, k, v, v_bias, same):
    weights = (jnp.exp2(nt_dot(q, k)) * same).astype(BF16)
    ones = jnp.ones((TOK, HD), BF16)
    mixed = jnp.dot(weights, jnp.concatenate([v, ones], 1), preferred_element_type=F32)
    return (mixed[:, :HD] / mixed[:, HD:] + v_bias).astype(BF16)


def whole_kernel(
    ny,
    nz,
    nx,
    dims_hbm,
    plan_hbm,
    feat_hbm,
    conv_hbm,
    embed_hbm,
    scale_hbm,
    shift_hbm,
    w_hbm,
    qg_hbm,
    kg_hbm,
    out_hbm,
    dims_ref,
    plan_ref,
    feat_ref,
    conv_ref,
    embed_ref,
    scale_ref,
    shift_ref,
    w_ref,
    qg_ref,
    kg_ref,
    stage,
    x_in,
    z_own,
    z_in,
    folds,
    x_all,
    out_ref,
    in_sem,
    sendx,
    recvx,
    sendz,
    recvz,
    sendy,
    recvy,
    sendq,
    recvq,
    sendo,
    recvo,
    out_sem,
    sendt,
    recvt,
    sendu,
    recvu,
):
    e = lax.axis_index("enc")
    s = lax.axis_index("seq")
    y, c = e // 2, mod(e, 2)
    z, x = s // nx, mod(s, nx)
    part_rows = LATF // nx
    fold_rows = 3 * part_rows

    def at_y(d):
        return {"enc": mod(y + d, ny) * 2 + c, "seq": s}

    def at_z(d):
        return {"enc": e, "seq": mod(z + d, nz) * nx + x}

    def at_x(d):
        return {"enc": e, "seq": z * nx + mod(x + d, nx)}

    sibling = {"enc": y * 2 + 1 - c, "seq": s}

    barrier = pltpu.get_barrier_semaphore()
    peers = [at_z(d) for d in reversed(near_first(nz))] + [at_y(d) for d in reversed(near_first(ny))]
    peers += [at_x(d) for d in reversed(near_first(nx))] + [sibling]
    for peer in peers:
        pl.semaphore_signal(barrier, inc=1, device_id=peer, device_id_type=MESH)

    loads = {}
    for i, (name, src, dst) in enumerate(
        [
            ("embed", embed_hbm, embed_ref),
            ("w", w_hbm, w_ref),
            ("scale", scale_hbm, scale_ref),
            ("shift", shift_hbm, shift_ref),
            ("dims", dims_hbm, dims_ref),
            ("plan", plan_hbm, plan_ref),
            ("conv", conv_hbm, conv_ref),
            ("feat", feat_hbm, feat_ref),
            ("qg", qg_hbm, qg_ref),
            ("kg", kg_hbm, kg_ref),
        ]
    ):
        loads[name] = pltpu.make_async_copy(src, dst, in_sem.at[i])
        loads[name].start()

    sends = []

    def send(src, dst, send_sem, recv_sem, peer):
        copy = pltpu.make_async_remote_copy(
            src_ref=src,
            dst_ref=dst,
            send_sem=send_sem,
            recv_sem=recv_sem,
            device_id=peer,
            device_id_type=MESH,
        )
        copy.start()
        sends.append(copy)
        return copy

    for name in ("embed", "w", "scale", "shift"):
        loads[name].wait()
    part = partial_fold(s, embed_ref, scale_ref, shift_ref, w_ref)
    row16 = lax.broadcasted_iota(jnp.int32, (16, HD), 0)
    bias = jnp.zeros((16, HD), F32)
    for j in range(3):
        bias = jnp.where(row16 == j, part[LATF : LATF + 16, j * HD : (j + 1) * HD], bias)
    bias = resplit(bias).astype(BF16)
    for g in range(nx):
        for j in range(3):
            stage[g, j * part_rows : (j + 1) * part_rows, :] = part[
                g * part_rows : (g + 1) * part_rows, j * HD : (j + 1) * HD
            ].astype(BF16)
        stage[g, fold_rows:, :] = bias

    for name in ("dims", "conv", "feat"):
        loads[name].wait()
    clip = (dims_ref[0, 0, 0], dims_ref[0, 0, 1], dims_ref[0, 0, 2])
    state = ([], jnp.zeros((LATF, TOK), F32))
    state = clip_frames(0, FC // 2, state, *clip, feat_ref, conv_ref)

    pl.semaphore_wait(barrier, len(peers))

    over_x = [
        send(stage.at[mod(x + d, nx)], x_in.at[d], sendx.at[d], recvx.at[d], at_x(d))
        for d in reversed(near_first(nx))
    ]

    state = clip_frames(FC // 2, FC, state, *clip, feat_ref, conv_ref)
    tokens = in_feature_order(state[1])
    _, count = token_places(*clip)
    loads["plan"].wait()
    for b in range(2):
        for i in range(4):
            x_all[e, 4 * b + i] = tokens[16 * i : 16 * i + 16, b * BLOCK : (b + 1) * BLOCK]
    owner0 = (jnp.zeros((16, BLOCK), jnp.int32) + plan_ref[0, 0, 0, 0]).astype(F32)
    owner1 = (jnp.zeros((16, BLOCK), jnp.int32) + plan_ref[0, 0, 1, 0]).astype(F32)
    meta = jnp.where(row16 == 0, owner0, jnp.where(row16 == 1, owner1, count[:, :BLOCK]))
    x_all[e, 8] = meta.astype(BF16)
    x_first = [
        send(x_all.at[e], x_all.at[e], sendt.at[d], recvt.at[d], at_y(d)) for d in near_first(ny)
    ]
    x_second = [send(x_all.at[e], x_all.at[e], sendu.at[0], recvu.at[0], sibling)]

    def finish(total):
        return jnp.concatenate([total[:fold_rows], resplit(total[fold_rows:])], 0).astype(BF16)

    total = stage[x].astype(F32)
    for copy in over_x:
        copy.wait_recv()
    for d in range(1, nx):
        total = total + x_in[d].astype(F32)
    z_own[...] = finish(total)
    over_z = [
        send(z_own, z_in.at[d], sendz.at[d], recvz.at[d], at_z(d))
        for d in reversed(near_first(nz))
    ]
    gram = gram_terms(embed_ref)

    def pass_tokens(d, copy):
        copy.wait_recv()
        source = mod(y - d + ny, ny) * 2 + c
        x_second.append(
            send(x_all.at[source], x_all.at[source], sendu.at[d], recvu.at[d], sibling)
        )

    arriving = list(zip(near_first(ny), x_first))
    early = len(arriving) // 2
    for d, copy in arriving[:early]:
        pass_tokens(d, copy)
    total = z_own[...].astype(F32)
    for copy in over_z:
        copy.wait_recv()
    for d in range(1, nz):
        total = total + z_in[d].astype(F32)
    folds[c, y, x] = finish(total)

    over_y = {}
    for d in near_first(ny):
        mine = folds.at[c, y, x]
        over_y[d] = send(mine, mine, sendy.at[d], recvy.at[d], at_y(d))
    quarters = {}

    def source_y(d):
        return mod(y - d + ny, ny)

    def spread(d):
        if d:
            over_y[d].wait_recv()
        piece = folds.at[c, source_y(d), x, pl.ds(0, fold_rows)]
        quarters[d] = [
            send(piece, piece, sendq.at[d, dx], recvq.at[d, dx], at_x(dx))
            for dx in near_first(nx)
        ]

    def arrived(d):
        for copy in quarters[d]:
            copy.wait_recv()

    crossed = []
    order = [0] + near_first(ny)
    spread(order[0])
    for d, copy in arriving[early:]:
        pass_tokens(d, copy)
    for d in order[1:]:
        spread(d)
    for copy in x_second:
        copy.wait_recv()
    inputs = [pick_clip(owner, 2 * ny, x_all, gram) for owner in (2 * y + 1 - c, e)]
    for name in ("qg", "kg"):
        loads[name].wait()
    gain = qg_ref[...] * kg_ref[...] * (HD**-0.5 * math.log2(math.e))
    stores = []

    def project(heads):
        projected = []
        for d, own in heads:
            keys, rows, _ = inputs[own]
            fold = [
                folds[c, source_y(d), :, j * part_rows : (j + 1) * part_rows, :].reshape(LATF, HD)
                for j in range(3)
            ]
            tail = folds[c, source_y(d), x, fold_rows:, :]
            projected.append(project_head(keys, rows, fold, tail, gain))
        return projected

    def mix(heads, projected):
        results = [
            mix_head(*parts, inputs[own][2]) for (d, own), parts in zip(heads, projected)
        ]
        for (d, own), result in zip(heads, results):
            out_ref[own, d] = result

    def deliver(heads):
        for d, own in heads:
            column = pl.ds(pl.multiple_of((2 * source_y(d) + c) * HD, HD), HD)
            target = out_hbm.at[:, column]
            if own:
                stores.append(pltpu.make_async_copy(out_ref.at[1, d], target, out_sem.at[d]))
                stores[-1].start()
            else:
                crossed.append(send(out_ref.at[0, d], target, sendo.at[d], recvo.at[d], sibling))

    first_half, second_half = order[: ny // 2 + 1], order[ny // 2 + 1 :]
    first = [(d, own) for own in (0, 1) for d in first_half]
    second = [(d, own) for own in (0, 1) for d in second_half]
    for d in first_half:
        arrived(d)
    mix(first, project(first))
    deliver(first)
    for d in second_half:
        arrived(d)
    second_parts = project(second)
    mix(second, second_parts)
    deliver(second)
    for copy in crossed:
        copy.wait_recv()
    for copy in stores:
        copy.wait()
    for copy in sends:
        copy.wait_send()


def whole(memory=pltpu.VMEM):
    return pl.BlockSpec(memory_space=memory)


def solution(mesh):
    ny = mesh.shape["enc"] // 2
    nx = 4 if mesh.shape["seq"] == 32 else 2
    nz = mesh.shape["seq"] // nx
    fold_rows = 3 * LATF // nx
    rows = fold_rows + 16
    dma = pltpu.SemaphoreType.DMA

    def on_device(
        clip_features,
        clip_shape,
        packing,
        conv_weight,
        embed_weight,
        mod_shift,
        mod_scale,
        qkv_weight,
        q_gain,
        k_gain,
    ):
        features = clip_features.shape[-1]
        width = embed_weight.shape[1]
        out = pl.pallas_call(
            functools.partial(whole_kernel, ny, nz, nx),
            out_shape=jax.ShapeDtypeStruct((BLOCK, 2 * ny * HD), BF16),
            in_specs=[whole(pltpu.HBM)] * 10,
            out_specs=whole(pltpu.HBM),
            scratch_shapes=[
                pltpu.SMEM((1, 1, 3), jnp.int32),
                pltpu.SMEM((1, 1, 2, 2), jnp.int32),
                pltpu.VMEM((FC * FRAME, features), BF16),
                pltpu.VMEM((27 * LAT, features), BF16),
                pltpu.VMEM((LATF, width), BF16),
                pltpu.VMEM((1, width), F32),
                pltpu.VMEM((1, width), F32),
                pltpu.VMEM(qkv_weight.shape, BF16),
                pltpu.VMEM((1, HD), F32),
                pltpu.VMEM((1, HD), F32),
                pltpu.VMEM((nx, rows, HD), BF16),
                pltpu.VMEM((nx, rows, HD), BF16),
                pltpu.VMEM((rows, HD), BF16),
                pltpu.VMEM((nz, rows, HD), BF16),
                pltpu.VMEM((2, ny, nx, rows, HD), BF16),
                pltpu.VMEM((2 * ny, 9, 16, BLOCK), BF16),
                pltpu.VMEM((2, ny, BLOCK, HD), BF16),
                dma((10,)),
                dma((nx,)),
                dma((nx,)),
                dma((nz,)),
                dma((nz,)),
                dma((ny,)),
                dma((ny,)),
                dma((ny, nx)),
                dma((ny, nx)),
                dma((ny,)),
                dma((ny,)),
                dma((ny,)),
                dma((ny,)),
                dma((ny,)),
                dma((ny,)),
                dma((ny,)),
            ],
            compiler_params=pltpu.CompilerParams(
                collective_id=0, has_side_effects=True, vmem_limit_bytes=60 * 1024 * 1024
            ),
            name="encode_move_attend",
        )(
            clip_shape,
            packing,
            clip_features.reshape(FC * FRAME, features),
            conv_weight.reshape(-1, features),
            embed_weight,
            mod_scale.reshape(1, -1),
            mod_shift.reshape(1, -1),
            qkv_weight,
            q_gain.reshape(1, -1),
            k_gain.reshape(1, -1),
        )
        return out[None]

    return jax.shard_map(
        on_device,
        mesh=mesh,
        in_specs=(
            P("enc", "seq", None, None, None, None),
            P("enc", "seq", None),
            P("enc", "seq", None, None),
            P(),
            P(),
            P(),
            P(),
            P(None, "seq", "enc"),
            P(),
            P(),
        ),
        out_specs=P("seq", "enc", None),
        check_vma=False,
    )
```

```python
import functools
import math

import jax
import jax.numpy as jnp
from jax import lax
from jax.experimental import pallas as pl
from jax.experimental.pallas import tpu as pltpu
from jax.sharding import PartitionSpec as P

MESH = pl.DeviceIdType.MESH
F32 = jnp.float32
BF16 = jnp.bfloat16
EPS = 1e-06
LATF = 64
LAT = 16
TOK = 256
BLOCK = 128
FRAME = 256
FC = 4
HD = 128


def mod(a, n):
    return lax.rem(a, n)


def near_first(n):
    order = []
    for d in range(1, n // 2 + 1):
        order.append(d)
        if n - d != d:
            order.append(n - d)
    return order


def split_bf16(value, terms):
    parts = []
    for _ in range(terms):
        part = value.astype(BF16)
        parts.append(part)
        value = value - part.astype(F32)
    return parts


def nt_dot(a, b):
    return lax.dot_general(a, b, (((1,), (1,)), ((), ())), preferred_element_type=F32)


def partial_fold(s, embed_ref, scale_ref, shift_ref, w_ref):
    embed = embed_ref[...].astype(F32)
    mean = jnp.mean(embed, -1, keepdims=True)
    window = pl.ds(pl.multiple_of((s // 2) * 128, 128), 128)
    a_part = (embed_ref[:, window].astype(F32) - mean) * (1.0 + scale_ref[:, window])
    shift_rows = jnp.broadcast_to(shift_ref[:, window], (16, 128))
    lhs = jnp.concatenate([a_part, shift_rows], 0)
    hi, lo = split_bf16(lhs, 2)
    lhs2 = jnp.concatenate([hi, lo], 1)
    half = lax.broadcasted_iota(jnp.int32, (128, 3 * HD), 0) // 64
    w_all = jnp.concatenate([w_ref[0], w_ref[1], w_ref[2]], 1).astype(F32)
    w_two = jnp.concatenate([w_all, w_all], 0)
    w_pad = jnp.where(half == mod(s, 2), w_two, 0.0).astype(BF16)
    rhs = jnp.concatenate([w_pad, w_pad], 0)
    return jnp.dot(lhs2, rhs, preferred_element_type=F32)


def token_places(frames, height, width):
    slot = lax.broadcasted_iota(jnp.int32, (1, TOK), 1).astype(F32)
    zero = jnp.zeros((1, TOK), jnp.int32)
    frames_v = (zero + frames).astype(F32)
    half_h = (zero + height).astype(F32) * 0.5
    half_w = (zero + width).astype(F32) * 0.5
    per_frame = half_h * half_w
    t = jnp.floor((slot + 0.5) / per_frame)
    within = slot - t * per_frame
    r = jnp.floor((within + 0.5) / half_w)
    q = within - r * half_w
    count = frames_v * per_frame
    return jnp.where(slot < count, t * FRAME + r * 32.0 + q * 2.0, -1.0), count


def clip_frames(first, last, state, frames, height, width, feat_ref, conv_ref):
    products, tokens = state
    lane = lax.broadcasted_iota(jnp.int32, (1, FRAME), 1)
    row, col = lane // 16, lane % 16
    inside = (row < height) & (col < width)
    conv = conv_ref[...]
    places, _ = token_places(frames, height, width)
    spot = lax.broadcasted_iota(jnp.int32, (FRAME, TOK), 0).astype(F32)
    taps = 9 * LAT
    for t in range(first, last):
        here = nt_dot(conv, feat_ref[t * FRAME : (t + 1) * FRAME, :])
        keep = inside & (lane < jnp.where(t < frames, FRAME, 0))
        products.append(jnp.where(keep, here, 0.0))
        summed = products[t][2 * taps :]
        if t >= 1:
            summed = summed + products[t - 1][taps : 2 * taps]
        if t >= 2:
            summed = summed + products[t - 2][:taps]
        third = 3 * LAT
        rows = summed[third : 2 * third]
        rows = rows + jnp.where(row >= 1, pltpu.roll(summed[:third], 16, 1), 0.0)
        rows = rows + jnp.where(row <= 14, pltpu.roll(summed[2 * third :], FRAME - 16, 1), 0.0)
        latent = rows[LAT : 2 * LAT]
        latent = latent + jnp.where(col >= 1, pltpu.roll(rows[:LAT], 1, 1), 0.0)
        latent = latent + jnp.where(col <= 14, pltpu.roll(rows[2 * LAT :], FRAME - 1, 1), 0.0)
        latent = latent.astype(BF16).astype(F32)
        phases = [latent] + [pltpu.roll(latent, FRAME - d, 1) for d in (1, 16, 17)]
        phases = jnp.concatenate(phases, 0).astype(BF16)
        pick = jnp.where(spot + float(t * FRAME) == places, 1.0, 0.0).astype(BF16)
        tokens = tokens + jnp.dot(phases, pick, preferred_element_type=F32)
    return products, tokens


def in_feature_order(tokens):
    out_row = lax.broadcasted_iota(jnp.int32, (LATF, LATF), 0)
    in_row = lax.broadcasted_iota(jnp.int32, (LATF, LATF), 1)
    swap = jnp.where(in_row == (out_row % 4) * LAT + out_row // 4, 1.0, 0.0).astype(BF16)
    return jnp.dot(swap, tokens.astype(BF16), preferred_element_type=F32).astype(BF16)


def gram_terms(embed_ref):
    embed = embed_ref[...]
    features = embed.shape[1]
    both = nt_dot(embed, embed)
    wide = embed.astype(F32)
    mean_col = jnp.mean(wide, -1, keepdims=True)
    ones = jnp.ones((8, features), BF16)
    mean_row = nt_dot(ones, embed)[:1] * (1.0 / features)
    gram = both * (1.0 / features) - mean_col * mean_row
    return jnp.concatenate(split_bf16(gram, 3), 0)


def resplit(tile):
    row = lax.broadcasted_iota(jnp.int32, tile.shape, 0)
    total = tile + pltpu.roll(tile, tile.shape[0] - 3, 0)
    high = total.astype(BF16).astype(F32)
    low = pltpu.roll(total - high, 3, 0)
    return jnp.where(row < 3, high, jnp.where(row < 6, low, 0.0))


def pick_clip(e, count, x_all, gram):
    chosen = jnp.zeros((2, 4, 16, BLOCK), F32)
    is1 = jnp.zeros((1, BLOCK), F32)
    live = jnp.zeros((1, BLOCK), F32)
    me = (jnp.zeros((1, BLOCK), jnp.int32) + e).astype(F32)
    for j in range(count):
        info = x_all[j, 8].astype(F32)
        here1 = jnp.where(info[1:2] == me, 1.0, 0.0)
        here = jnp.where(info[0:1] == me, 1.0, 0.0) + here1
        is1 = is1 + here1
        live = live + here * info[2:3]
        chosen = chosen + x_all[j, 0:8].astype(F32).reshape(2, 4, 16, BLOCK) * here
    chosen = chosen.reshape(2, LATF, BLOCK)
    xt = jnp.concatenate([chosen[0].T, chosen[1].T], 0)
    xt16 = xt.astype(BF16)
    mixed = jnp.dot(jnp.concatenate([xt16, xt16, xt16], 1), gram, preferred_element_type=F32)
    var = jnp.sum(mixed * xt, -1, keepdims=True)
    scaled = xt * lax.rsqrt(jnp.maximum(var, 0.0) + EPS)
    high, low = split_bf16(scaled, 2)
    keys = jnp.concatenate([high, low], 1)
    rows = jnp.where(is1 > 0.5, keys[BLOCK:].astype(F32), keys[:BLOCK].astype(F32)).astype(BF16)
    q_slot = lax.broadcasted_iota(jnp.int32, (BLOCK, BLOCK), 0).astype(F32) + is1 * BLOCK
    q_live = jnp.where(q_slot < live, 1.0, 0.0)
    same = []
    for b in range(2):
        k_slot = lax.broadcasted_iota(jnp.int32, (1, BLOCK), 1).astype(F32) + float(b * BLOCK)
        k_live = jnp.where(k_slot < live, 1.0, 0.0)
        same.append(jnp.where(q_live == k_live, 1.0, 0.0))
    return keys, rows, jnp.concatenate(same, 1)


def project_head(keys, rows, fold, tail, gain):
    tail = tail.astype(F32)
    bias = tail[0:3] + tail[3:6]
    q_fold = jnp.concatenate([fold[0], fold[0]], 0)
    kv_fold = jnp.concatenate(fold[1:], 1)
    q = jnp.dot(rows, q_fold, preferred_element_type=F32) + bias[0:1]
    kv = jnp.dot(keys, jnp.concatenate([kv_fold, kv_fold], 0), preferred_element_type=F32)
    k = kv[:, :HD] + bias[1:2]
    q = q * lax.rsqrt(jnp.mean(q * q, -1, keepdims=True) + EPS) * gain
    k = k * lax.rsqrt(jnp.mean(k * k, -1, keepdims=True) + EPS)
    return q.astype(BF16), k.astype(BF16), kv[:, HD:].astype(BF16), bias[2:3]


def mix_head(q, k, v, v_bias, same):
    weights = (jnp.exp2(nt_dot(q, k)) * same).astype(BF16)
    ones = jnp.ones((TOK, HD), BF16)
    mixed = jnp.dot(weights, jnp.concatenate([v, ones], 1), preferred_element_type=F32)
    return (mixed[:, :HD] / mixed[:, HD:] + v_bias).astype(BF16)


def whole_kernel(
    ny,
    nz,
    nx,
    dims_hbm,
    plan_hbm,
    feat_hbm,
    conv_hbm,
    embed_hbm,
    scale_hbm,
    shift_hbm,
    w_hbm,
    qg_hbm,
    kg_hbm,
    out_ref,
    dims_ref,
    plan_ref,
    feat_ref,
    conv_ref,
    embed_ref,
    scale_ref,
    shift_ref,
    w_ref,
    qg_ref,
    kg_ref,
    stage,
    x_in,
    z_own,
    z_in,
    folds,
    x_all,
    crossing,
    in_sem,
    sendx,
    recvx,
    sendz,
    recvz,
    sendy,
    recvy,
    sendq,
    recvq,
    sendo,
    recvo,
    sendt,
    recvt,
    sendu,
    recvu,
):
    e = lax.axis_index("enc")
    s = lax.axis_index("seq")
    y, c = e // 2, mod(e, 2)
    z, x = s // nx, mod(s, nx)
    part_rows = LATF // nx
    fold_rows = 3 * part_rows

    def at_y(d):
        return {"enc": mod(y + d, ny) * 2 + c, "seq": s}

    def at_z(d):
        return {"enc": e, "seq": mod(z + d, nz) * nx + x}

    def at_x(d):
        return {"enc": e, "seq": z * nx + mod(x + d, nx)}

    sibling = {"enc": y * 2 + 1 - c, "seq": s}

    barrier = pltpu.get_barrier_semaphore()
    peers = [at_z(d) for d in reversed(near_first(nz))] + [at_y(d) for d in reversed(near_first(ny))]
    peers += [at_x(d) for d in reversed(near_first(nx))] + [sibling]
    for peer in peers:
        pl.semaphore_signal(barrier, inc=1, device_id=peer, device_id_type=MESH)

    loads = {}
    for i, (name, src, dst) in enumerate(
        [
            ("embed", embed_hbm, embed_ref),
            ("w", w_hbm, w_ref),
            ("scale", scale_hbm, scale_ref),
            ("shift", shift_hbm, shift_ref),
            ("dims", dims_hbm, dims_ref),
            ("plan", plan_hbm, plan_ref),
            ("conv", conv_hbm, conv_ref),
            ("feat", feat_hbm, feat_ref),
            ("qg", qg_hbm, qg_ref),
            ("kg", kg_hbm, kg_ref),
        ]
    ):
        loads[name] = pltpu.make_async_copy(src, dst, in_sem.at[i])
        loads[name].start()

    sends = []

    def send(src, dst, send_sem, recv_sem, peer):
        copy = pltpu.make_async_remote_copy(
            src_ref=src,
            dst_ref=dst,
            send_sem=send_sem,
            recv_sem=recv_sem,
            device_id=peer,
            device_id_type=MESH,
        )
        copy.start()
        sends.append(copy)
        return copy

    for name in ("embed", "w", "scale", "shift"):
        loads[name].wait()
    part = partial_fold(s, embed_ref, scale_ref, shift_ref, w_ref)
    row16 = lax.broadcasted_iota(jnp.int32, (16, HD), 0)
    bias = jnp.zeros((16, HD), F32)
    for j in range(3):
        bias = jnp.where(row16 == j, part[LATF : LATF + 16, j * HD : (j + 1) * HD], bias)
    bias = resplit(bias).astype(BF16)
    for g in range(nx):
        for j in range(3):
            stage[g, j * part_rows : (j + 1) * part_rows, :] = part[
                g * part_rows : (g + 1) * part_rows, j * HD : (j + 1) * HD
            ].astype(BF16)
        stage[g, fold_rows:, :] = bias

    for name in ("dims", "conv", "feat"):
        loads[name].wait()
    clip = (dims_ref[0, 0, 0], dims_ref[0, 0, 1], dims_ref[0, 0, 2])
    state = ([], jnp.zeros((LATF, TOK), F32))
    state = clip_frames(0, FC // 2, state, *clip, feat_ref, conv_ref)

    pl.semaphore_wait(barrier, len(peers))

    over_x = [
        send(stage.at[mod(x + d, nx)], x_in.at[d], sendx.at[d], recvx.at[d], at_x(d))
        for d in reversed(near_first(nx))
    ]

    state = clip_frames(FC // 2, FC, state, *clip, feat_ref, conv_ref)
    tokens = in_feature_order(state[1])
    _, count = token_places(*clip)
    loads["plan"].wait()
    for b in range(2):
        for i in range(4):
            x_all[e, 4 * b + i] = tokens[16 * i : 16 * i + 16, b * BLOCK : (b + 1) * BLOCK]
    owner0 = (jnp.zeros((16, BLOCK), jnp.int32) + plan_ref[0, 0, 0, 0]).astype(F32)
    owner1 = (jnp.zeros((16, BLOCK), jnp.int32) + plan_ref[0, 0, 1, 0]).astype(F32)
    meta = jnp.where(row16 == 0, owner0, jnp.where(row16 == 1, owner1, count[:, :BLOCK]))
    x_all[e, 8] = meta.astype(BF16)
    x_first = [
        send(x_all.at[e], x_all.at[e], sendt.at[d], recvt.at[d], at_y(d)) for d in near_first(ny)
    ]
    x_second = [send(x_all.at[e], x_all.at[e], sendu.at[0], recvu.at[0], sibling)]

    def finish(total):
        return jnp.concatenate([total[:fold_rows], resplit(total[fold_rows:])], 0).astype(BF16)

    total = stage[x].astype(F32)
    for copy in over_x:
        copy.wait_recv()
    for d in range(1, nx):
        total = total + x_in[d].astype(F32)
    z_own[...] = finish(total)
    over_z = [
        send(z_own, z_in.at[d], sendz.at[d], recvz.at[d], at_z(d))
        for d in reversed(near_first(nz))
    ]
    gram = gram_terms(embed_ref)

    def pass_tokens(d, copy):
        copy.wait_recv()
        source = mod(y - d + ny, ny) * 2 + c
        x_second.append(
            send(x_all.at[source], x_all.at[source], sendu.at[d], recvu.at[d], sibling)
        )

    arriving = list(zip(near_first(ny), x_first))
    early = len(arriving) // 2
    for d, copy in arriving[:early]:
        pass_tokens(d, copy)
    total = z_own[...].astype(F32)
    for copy in over_z:
        copy.wait_recv()
    for d in range(1, nz):
        total = total + z_in[d].astype(F32)
    folds[c, y, x] = finish(total)

    over_y = {}
    for d in near_first(ny):
        mine = folds.at[c, y, x]
        over_y[d] = send(mine, mine, sendy.at[d], recvy.at[d], at_y(d))
    quarters = {}

    def source_y(d):
        return mod(y - d + ny, ny)

    def spread(d):
        if d:
            over_y[d].wait_recv()
        piece = folds.at[c, source_y(d), x, pl.ds(0, fold_rows)]
        quarters[d] = [
            send(piece, piece, sendq.at[d, dx], recvq.at[d, dx], at_x(dx))
            for dx in near_first(nx)
        ]

    def arrived(d):
        for copy in quarters[d]:
            copy.wait_recv()

    crossed = []
    order = [0] + near_first(ny)
    spread(order[0])
    for d, copy in arriving[early:]:
        pass_tokens(d, copy)
    for d in order[1:]:
        spread(d)
    for copy in x_second:
        copy.wait_recv()
    inputs = [pick_clip(owner, 2 * ny, x_all, gram) for owner in (2 * y + 1 - c, e)]
    for name in ("qg", "kg"):
        loads[name].wait()
    gain = qg_ref[...] * kg_ref[...] * (HD**-0.5 * math.log2(math.e))

    def project(heads):
        projected = []
        for d, own in heads:
            keys, rows, _ = inputs[own]
            fold = [
                folds[c, source_y(d), :, j * part_rows : (j + 1) * part_rows, :].reshape(LATF, HD)
                for j in range(3)
            ]
            tail = folds[c, source_y(d), x, fold_rows:, :]
            projected.append(project_head(keys, rows, fold, tail, gain))
        return projected

    def mix(heads, projected):
        results = [
            mix_head(*parts, inputs[own][2]) for (d, own), parts in zip(heads, projected)
        ]
        for (d, own), result in zip(heads, results):
            column = pl.ds(pl.multiple_of((2 * source_y(d) + c) * HD, HD), HD)
            if own:
                out_ref[:, column] = result
            else:
                crossing[d] = result
                target = out_ref.at[:, column]
                crossed.append(send(crossing.at[d], target, sendo.at[d], recvo.at[d], sibling))

    first_half, second_half = order[: ny // 2 + 1], order[ny // 2 + 1 :]
    first = [(d, own) for own in (0, 1) for d in first_half]
    second = [(d, own) for own in (0, 1) for d in second_half]
    for d in first_half:
        arrived(d)
    mix(first, project(first))
    for d in second_half:
        arrived(d)
    second_parts = project(second)
    mix(second, second_parts)
    for copy in crossed:
        copy.wait_recv()
    for copy in sends:
        copy.wait_send()


def whole(memory=pltpu.VMEM):
    return pl.BlockSpec(memory_space=memory)


def solution(mesh):
    ny = mesh.shape["enc"] // 2
    nx = 4 if mesh.shape["seq"] == 32 else 2
    nz = mesh.shape["seq"] // nx
    fold_rows = 3 * LATF // nx
    rows = fold_rows + 16
    dma = pltpu.SemaphoreType.DMA

    def on_device(
        clip_features,
        clip_shape,
        packing,
        conv_weight,
        embed_weight,
        mod_shift,
        mod_scale,
        qkv_weight,
        q_gain,
        k_gain,
    ):
        features = clip_features.shape[-1]
        width = embed_weight.shape[1]
        out = pl.pallas_call(
            functools.partial(whole_kernel, ny, nz, nx),
            out_shape=pltpu.VMEM((BLOCK, 2 * ny * HD), BF16),
            in_specs=[whole(pltpu.HBM)] * 10,
            out_specs=whole(),
            scratch_shapes=[
                pltpu.SMEM((1, 1, 3), jnp.int32),
                pltpu.SMEM((1, 1, 2, 2), jnp.int32),
                pltpu.VMEM((FC * FRAME, features), BF16),
                pltpu.VMEM((27 * LAT, features), BF16),
                pltpu.VMEM((LATF, width), BF16),
                pltpu.VMEM((1, width), F32),
                pltpu.VMEM((1, width), F32),
                pltpu.VMEM(qkv_weight.shape, BF16),
                pltpu.VMEM((1, HD), F32),
                pltpu.VMEM((1, HD), F32),
                pltpu.VMEM((nx, rows, HD), BF16),
                pltpu.VMEM((nx, rows, HD), BF16),
                pltpu.VMEM((rows, HD), BF16),
                pltpu.VMEM((nz, rows, HD), BF16),
                pltpu.VMEM((2, ny, nx, rows, HD), BF16),
                pltpu.VMEM((2 * ny, 9, 16, BLOCK), BF16),
                pltpu.VMEM((ny, BLOCK, HD), BF16),
                dma((10,)),
                dma((nx,)),
                dma((nx,)),
                dma((nz,)),
                dma((nz,)),
                dma((ny,)),
                dma((ny,)),
                dma((ny, nx)),
                dma((ny, nx)),
                dma((ny,)),
                dma((ny,)),
                dma((ny,)),
                dma((ny,)),
                dma((ny,)),
                dma((ny,)),
            ],
            compiler_params=pltpu.CompilerParams(
                collective_id=0, has_side_effects=True, vmem_limit_bytes=60 * 1024 * 1024
            ),
            name="encode_move_attend",
        )(
            clip_shape,
            packing,
            clip_features.reshape(FC * FRAME, features),
            conv_weight.reshape(-1, features),
            embed_weight,
            mod_scale.reshape(1, -1),
            mod_shift.reshape(1, -1),
            qkv_weight,
            q_gain.reshape(1, -1),
            k_gain.reshape(1, -1),
        )
        return out[None]

    return jax.shard_map(
        on_device,
        mesh=mesh,
        in_specs=(
            P("enc", "seq", None, None, None, None),
            P("enc", "seq", None),
            P("enc", "seq", None, None),
            P(),
            P(),
            P(),
            P(),
            P(None, "seq", "enc"),
            P(),
            P(),
        ),
        out_specs=P("seq", "enc", None),
        check_vma=False,
    )
```

```python
import functools
import math

import jax
import jax.numpy as jnp
from jax import lax
from jax.experimental import pallas as pl
from jax.experimental.pallas import tpu as pltpu
from jax.sharding import PartitionSpec as P

MESH = pl.DeviceIdType.MESH
F32 = jnp.float32
BF16 = jnp.bfloat16
EPS = 1e-06
LATF = 64
LAT = 16
TOK = 256
BLOCK = 128
FRAME = 256
FC = 4
HD = 128


def mod(a, n):
    return lax.rem(a, n)


def near_first(n):
    order = []
    for d in range(1, n // 2 + 1):
        order.append(d)
        if n - d != d:
            order.append(n - d)
    return order


def split_bf16(value, terms):
    parts = []
    for _ in range(terms):
        part = value.astype(BF16)
        parts.append(part)
        value = value - part.astype(F32)
    return parts


def nt_dot(a, b):
    return lax.dot_general(a, b, (((1,), (1,)), ((), ())), preferred_element_type=F32)


def partial_fold(s, embed_ref, scale_ref, shift_ref, w_ref):
    embed = embed_ref[...].astype(F32)
    mean = jnp.mean(embed, -1, keepdims=True)
    window = pl.ds(pl.multiple_of((s // 2) * 128, 128), 128)
    a_part = (embed_ref[:, window].astype(F32) - mean) * (1.0 + scale_ref[:, window])
    shift_rows = jnp.broadcast_to(shift_ref[:, window], (16, 128))
    lhs = jnp.concatenate([a_part, shift_rows], 0)
    hi, lo = split_bf16(lhs, 2)
    lhs2 = jnp.concatenate([hi, lo], 1)
    half = lax.broadcasted_iota(jnp.int32, (128, 3 * HD), 0) // 64
    w_all = jnp.concatenate([w_ref[0], w_ref[1], w_ref[2]], 1).astype(F32)
    w_two = jnp.concatenate([w_all, w_all], 0)
    w_pad = jnp.where(half == mod(s, 2), w_two, 0.0).astype(BF16)
    rhs = jnp.concatenate([w_pad, w_pad], 0)
    return jnp.dot(lhs2, rhs, preferred_element_type=F32)


def token_places(frames, height, width):
    slot = lax.broadcasted_iota(jnp.int32, (1, TOK), 1).astype(F32)
    zero = jnp.zeros((1, TOK), jnp.int32)
    frames_v = (zero + frames).astype(F32)
    half_h = (zero + height).astype(F32) * 0.5
    half_w = (zero + width).astype(F32) * 0.5
    per_frame = half_h * half_w
    t = jnp.floor((slot + 0.5) / per_frame)
    within = slot - t * per_frame
    r = jnp.floor((within + 0.5) / half_w)
    q = within - r * half_w
    count = frames_v * per_frame
    return jnp.where(slot < count, t * FRAME + r * 32.0 + q * 2.0, -1.0), count


def clip_frames(first, last, state, frames, height, width, feat_ref, conv_ref):
    products, tokens = state
    lane = lax.broadcasted_iota(jnp.int32, (1, FRAME), 1)
    row, col = lane // 16, lane % 16
    inside = (row < height) & (col < width)
    conv = conv_ref[...]
    places, _ = token_places(frames, height, width)
    spot = lax.broadcasted_iota(jnp.int32, (FRAME, TOK), 0).astype(F32)
    taps = 9 * LAT
    for t in range(first, last):
        here = nt_dot(conv, feat_ref[t * FRAME : (t + 1) * FRAME, :])
        keep = inside & (lane < jnp.where(t < frames, FRAME, 0))
        products.append(jnp.where(keep, here, 0.0))
        summed = products[t][2 * taps :]
        if t >= 1:
            summed = summed + products[t - 1][taps : 2 * taps]
        if t >= 2:
            summed = summed + products[t - 2][:taps]
        third = 3 * LAT
        rows = summed[third : 2 * third]
        rows = rows + jnp.where(row >= 1, pltpu.roll(summed[:third], 16, 1), 0.0)
        rows = rows + jnp.where(row <= 14, pltpu.roll(summed[2 * third :], FRAME - 16, 1), 0.0)
        latent = rows[LAT : 2 * LAT]
        latent = latent + jnp.where(col >= 1, pltpu.roll(rows[:LAT], 1, 1), 0.0)
        latent = latent + jnp.where(col <= 14, pltpu.roll(rows[2 * LAT :], FRAME - 1, 1), 0.0)
        latent = latent.astype(BF16).astype(F32)
        phases = [latent] + [pltpu.roll(latent, FRAME - d, 1) for d in (1, 16, 17)]
        phases = jnp.concatenate(phases, 0).astype(BF16)
        pick = jnp.where(spot + float(t * FRAME) == places, 1.0, 0.0).astype(BF16)
        tokens = tokens + jnp.dot(phases, pick, preferred_element_type=F32)
    return products, tokens


def in_feature_order(tokens):
    out_row = lax.broadcasted_iota(jnp.int32, (LATF, LATF), 0)
    in_row = lax.broadcasted_iota(jnp.int32, (LATF, LATF), 1)
    swap = jnp.where(in_row == (out_row % 4) * LAT + out_row // 4, 1.0, 0.0).astype(BF16)
    return jnp.dot(swap, tokens.astype(BF16), preferred_element_type=F32).astype(BF16)


def gram_terms(embed_ref):
    embed = embed_ref[...]
    features = embed.shape[1]
    both = nt_dot(embed, embed)
    wide = embed.astype(F32)
    mean_col = jnp.mean(wide, -1, keepdims=True)
    ones = jnp.ones((8, features), BF16)
    mean_row = nt_dot(ones, embed)[:1] * (1.0 / features)
    gram = both * (1.0 / features) - mean_col * mean_row
    return jnp.concatenate(split_bf16(gram, 3), 0)


def resplit(tile):
    row = lax.broadcasted_iota(jnp.int32, tile.shape, 0)
    total = tile + pltpu.roll(tile, tile.shape[0] - 3, 0)
    high = total.astype(BF16).astype(F32)
    low = pltpu.roll(total - high, 3, 0)
    return jnp.where(row < 3, high, jnp.where(row < 6, low, 0.0))


def pick_clip(e, count, x_all, gram):
    chosen = jnp.zeros((2, 4, 16, BLOCK), F32)
    is1 = jnp.zeros((1, BLOCK), F32)
    live = jnp.zeros((1, BLOCK), F32)
    me = (jnp.zeros((1, BLOCK), jnp.int32) + e).astype(F32)
    for j in range(count):
        info = x_all[j, 8].astype(F32)
        here1 = jnp.where(info[1:2] == me, 1.0, 0.0)
        here = jnp.where(info[0:1] == me, 1.0, 0.0) + here1
        is1 = is1 + here1
        live = live + here * info[2:3]
        chosen = chosen + x_all[j, 0:8].astype(F32).reshape(2, 4, 16, BLOCK) * here
    chosen = chosen.reshape(2, LATF, BLOCK)
    xt = jnp.concatenate([chosen[0].T, chosen[1].T], 0)
    xt16 = xt.astype(BF16)
    mixed = jnp.dot(jnp.concatenate([xt16, xt16, xt16], 1), gram, preferred_element_type=F32)
    var = jnp.sum(mixed * xt, -1, keepdims=True)
    scaled = xt * lax.rsqrt(jnp.maximum(var, 0.0) + EPS)
    high, low = split_bf16(scaled, 2)
    keys = jnp.concatenate([high, low], 1)
    rows = jnp.where(is1 > 0.5, keys[BLOCK:].astype(F32), keys[:BLOCK].astype(F32)).astype(BF16)
    q_slot = lax.broadcasted_iota(jnp.int32, (BLOCK, BLOCK), 0).astype(F32) + is1 * BLOCK
    q_live = jnp.where(q_slot < live, 1.0, 0.0)
    same = []
    for b in range(2):
        k_slot = lax.broadcasted_iota(jnp.int32, (1, BLOCK), 1).astype(F32) + float(b * BLOCK)
        k_live = jnp.where(k_slot < live, 1.0, 0.0)
        same.append(jnp.where(q_live == k_live, 1.0, 0.0))
    return keys, rows, jnp.concatenate(same, 1)


def project_head(keys, rows, fold, tail, gain):
    tail = tail.astype(F32)
    bias = tail[0:3] + tail[3:6]
    q_fold = jnp.concatenate([fold[0], fold[0]], 0)
    kv_fold = jnp.concatenate(fold[1:], 1)
    q = jnp.dot(rows, q_fold, preferred_element_type=F32) + bias[0:1]
    kv = jnp.dot(keys, jnp.concatenate([kv_fold, kv_fold], 0), preferred_element_type=F32)
    k = kv[:, :HD] + bias[1:2]
    q = q * lax.rsqrt(jnp.mean(q * q, -1, keepdims=True) + EPS) * gain
    k = k * lax.rsqrt(jnp.mean(k * k, -1, keepdims=True) + EPS)
    return q.astype(BF16), k.astype(BF16), kv[:, HD:].astype(BF16), bias[2:3]


def mix_head(q, k, v, v_bias, same):
    weights = (jnp.exp2(nt_dot(q, k)) * same).astype(BF16)
    ones = jnp.ones((TOK, HD), BF16)
    mixed = jnp.dot(weights, jnp.concatenate([v, ones], 1), preferred_element_type=F32)
    return (mixed[:, :HD] / mixed[:, HD:] + v_bias).astype(BF16)


def whole_kernel(
    ny,
    nz,
    nx,
    dims_hbm,
    plan_hbm,
    feat_hbm,
    conv_hbm,
    embed_hbm,
    scale_hbm,
    shift_hbm,
    w_hbm,
    qg_hbm,
    kg_hbm,
    out_ref,
    dims_ref,
    plan_ref,
    feat_ref,
    conv_ref,
    embed_ref,
    scale_ref,
    shift_ref,
    w_ref,
    qg_ref,
    kg_ref,
    stage,
    x_in,
    z_own,
    z_in,
    folds,
    x_all,
    crossing,
    in_sem,
    sendx,
    recvx,
    sendz,
    recvz,
    sendy,
    recvy,
    sendq,
    recvq,
    sendo,
    recvo,
    sendt,
    recvt,
    sendu,
    recvu,
):
    e = lax.axis_index("enc")
    s = lax.axis_index("seq")
    y, c = e // 2, mod(e, 2)
    z, x = s // nx, mod(s, nx)
    part_rows = LATF // nx
    fold_rows = 3 * part_rows

    def at_y(d):
        return {"enc": mod(y + d, ny) * 2 + c, "seq": s}

    def at_z(d):
        return {"enc": e, "seq": mod(z + d, nz) * nx + x}

    def at_x(d):
        return {"enc": e, "seq": z * nx + mod(x + d, nx)}

    sibling = {"enc": y * 2 + 1 - c, "seq": s}

    barrier = pltpu.get_barrier_semaphore()
    peers = [at_z(d) for d in reversed(near_first(nz))] + [at_y(d) for d in reversed(near_first(ny))]
    peers += [at_x(d) for d in reversed(near_first(nx))] + [sibling]
    for peer in peers:
        pl.semaphore_signal(barrier, inc=1, device_id=peer, device_id_type=MESH)

    loads = {}
    for i, (name, src, dst) in enumerate(
        [
            ("embed", embed_hbm, embed_ref),
            ("w", w_hbm, w_ref),
            ("scale", scale_hbm, scale_ref),
            ("shift", shift_hbm, shift_ref),
            ("dims", dims_hbm, dims_ref),
            ("plan", plan_hbm, plan_ref),
            ("conv", conv_hbm, conv_ref),
            ("feat", feat_hbm, feat_ref),
            ("qg", qg_hbm, qg_ref),
            ("kg", kg_hbm, kg_ref),
        ]
    ):
        loads[name] = pltpu.make_async_copy(src, dst, in_sem.at[i])
        loads[name].start()

    def settle(copies):
        for copy in copies:
            copy.wait_send()

    def send(src, dst, send_sem, recv_sem, peer):
        copy = pltpu.make_async_remote_copy(
            src_ref=src,
            dst_ref=dst,
            send_sem=send_sem,
            recv_sem=recv_sem,
            device_id=peer,
            device_id_type=MESH,
        )
        copy.start()
        return copy

    for name in ("embed", "w", "scale", "shift"):
        loads[name].wait()
    part = partial_fold(s, embed_ref, scale_ref, shift_ref, w_ref)
    row16 = lax.broadcasted_iota(jnp.int32, (16, HD), 0)
    bias = jnp.zeros((16, HD), F32)
    for j in range(3):
        bias = jnp.where(row16 == j, part[LATF : LATF + 16, j * HD : (j + 1) * HD], bias)
    bias = resplit(bias).astype(BF16)
    for g in range(nx):
        for j in range(3):
            stage[g, j * part_rows : (j + 1) * part_rows, :] = part[
                g * part_rows : (g + 1) * part_rows, j * HD : (j + 1) * HD
            ].astype(BF16)
        stage[g, fold_rows:, :] = bias

    for name in ("dims", "conv", "feat"):
        loads[name].wait()
    clip = (dims_ref[0, 0, 0], dims_ref[0, 0, 1], dims_ref[0, 0, 2])
    state = ([], jnp.zeros((LATF, TOK), F32))
    state = clip_frames(0, FC // 2, state, *clip, feat_ref, conv_ref)

    pl.semaphore_wait(barrier, len(peers))

    over_x = [
        send(stage.at[mod(x + d, nx)], x_in.at[d], sendx.at[d], recvx.at[d], at_x(d))
        for d in reversed(near_first(nx))
    ]

    state = clip_frames(FC // 2, FC, state, *clip, feat_ref, conv_ref)
    tokens = in_feature_order(state[1])
    _, count = token_places(*clip)
    loads["plan"].wait()
    for b in range(2):
        for i in range(4):
            x_all[e, 4 * b + i] = tokens[16 * i : 16 * i + 16, b * BLOCK : (b + 1) * BLOCK]
    owner0 = (jnp.zeros((16, BLOCK), jnp.int32) + plan_ref[0, 0, 0, 0]).astype(F32)
    owner1 = (jnp.zeros((16, BLOCK), jnp.int32) + plan_ref[0, 0, 1, 0]).astype(F32)
    meta = jnp.where(row16 == 0, owner0, jnp.where(row16 == 1, owner1, count[:, :BLOCK]))
    x_all[e, 8] = meta.astype(BF16)
    x_first = [
        send(x_all.at[e], x_all.at[e], sendt.at[d], recvt.at[d], at_y(d)) for d in near_first(ny)
    ]
    x_second = [send(x_all.at[e], x_all.at[e], sendu.at[0], recvu.at[0], sibling)]

    def finish(total):
        return jnp.concatenate([total[:fold_rows], resplit(total[fold_rows:])], 0).astype(BF16)

    total = stage[x].astype(F32)
    for copy in over_x:
        copy.wait_recv()
    for d in range(1, nx):
        total = total + x_in[d].astype(F32)
    z_own[...] = finish(total)
    over_z = [
        send(z_own, z_in.at[d], sendz.at[d], recvz.at[d], at_z(d))
        for d in reversed(near_first(nz))
    ]
    gram = gram_terms(embed_ref)

    def pass_tokens(d, copy):
        copy.wait_recv()
        source = mod(y - d + ny, ny) * 2 + c
        x_second.append(
            send(x_all.at[source], x_all.at[source], sendu.at[d], recvu.at[d], sibling)
        )

    arriving = list(zip(near_first(ny), x_first))
    early = len(arriving) // 2
    for d, copy in arriving[:early]:
        pass_tokens(d, copy)
    total = z_own[...].astype(F32)
    for copy in over_z:
        copy.wait_recv()
    for d in range(1, nz):
        total = total + z_in[d].astype(F32)
    folds[c, y, x] = finish(total)

    over_y = {}
    for d in ([1, 7, 2, 6, 4, 3, 5] if ny == 8 else near_first(ny)):
        mine = folds.at[c, y, x]
        over_y[d] = send(mine, mine, sendy.at[d], recvy.at[d], at_y(d))
    quarters = {}

    def source_y(d):
        return mod(y - d + ny, ny)

    def spread(d):
        if d:
            over_y[d].wait_recv()
        piece = folds.at[c, source_y(d), x, pl.ds(0, fold_rows)]
        quarters[d] = [
            send(piece, piece, sendq.at[d, dx], recvq.at[d, dx], at_x(dx))
            for dx in near_first(nx)
        ]

    def arrived(d):
        for copy in quarters[d]:
            copy.wait_recv()

    crossed = []
    order = [0] + near_first(ny)
    spread(order[0])
    for d, copy in arriving[early:]:
        pass_tokens(d, copy)
    for d in order[1:]:
        spread(d)
    settle(over_x + over_z + list(over_y.values()) + x_first)
    for copy in x_second:
        copy.wait_recv()
    settle(x_second)
    inputs = [pick_clip(owner, 2 * ny, x_all, gram) for owner in (2 * y + 1 - c, e)]
    for name in ("qg", "kg"):
        loads[name].wait()
    gain = qg_ref[...] * kg_ref[...] * (HD**-0.5 * math.log2(math.e))

    def project(heads):
        projected = []
        for d, own in heads:
            keys, rows, _ = inputs[own]
            fold = [
                folds[c, source_y(d), :, j * part_rows : (j + 1) * part_rows, :].reshape(LATF, HD)
                for j in range(3)
            ]
            tail = folds[c, source_y(d), x, fold_rows:, :]
            projected.append(project_head(keys, rows, fold, tail, gain))
        return projected

    def mix(heads, projected):
        results = [
            mix_head(*parts, inputs[own][2]) for (d, own), parts in zip(heads, projected)
        ]
        for (d, own), result in zip(heads, results):
            column = pl.ds(pl.multiple_of((2 * source_y(d) + c) * HD, HD), HD)
            if own:
                out_ref[:, column] = result
            else:
                crossing[d] = result
                target = out_ref.at[:, column]
                crossed.append(send(crossing.at[d], target, sendo.at[d], recvo.at[d], sibling))

    first_half, second_half = order[: ny // 2 + 1], order[ny // 2 + 1 :]
    first = [(d, own) for own in (0, 1) for d in first_half]
    second = [(d, own) for own in (0, 1) for d in second_half]
    for d in first_half:
        arrived(d)
    mix(first, project(first))
    for d in second_half:
        arrived(d)
    second_parts = project(second)
    count = len(second_half)
    mix(second[:count], second_parts[:count])
    for d in order:
        settle(quarters[d])
    mix(second[count:], second_parts[count:])
    for copy in crossed:
        copy.wait_recv()
    settle(crossed)


def whole(memory=pltpu.VMEM):
    return pl.BlockSpec(memory_space=memory)


def solution(mesh):
    ny = mesh.shape["enc"] // 2
    nx = 4 if mesh.shape["seq"] == 32 else 2
    nz = mesh.shape["seq"] // nx
    fold_rows = 3 * LATF // nx
    rows = fold_rows + 16
    dma = pltpu.SemaphoreType.DMA

    def on_device(
        clip_features,
        clip_shape,
        packing,
        conv_weight,
        embed_weight,
        mod_shift,
        mod_scale,
        qkv_weight,
        q_gain,
        k_gain,
    ):
        features = clip_features.shape[-1]
        width = embed_weight.shape[1]
        out = pl.pallas_call(
            functools.partial(whole_kernel, ny, nz, nx),
            out_shape=pltpu.VMEM((BLOCK, 2 * ny * HD), BF16),
            in_specs=[whole(pltpu.HBM)] * 10,
            out_specs=whole(),
            scratch_shapes=[
                pltpu.SMEM((1, 1, 3), jnp.int32),
                pltpu.SMEM((1, 1, 2, 2), jnp.int32),
                pltpu.VMEM((FC * FRAME, features), BF16),
                pltpu.VMEM((27 * LAT, features), BF16),
                pltpu.VMEM((LATF, width), BF16),
                pltpu.VMEM((1, width), F32),
                pltpu.VMEM((1, width), F32),
                pltpu.VMEM(qkv_weight.shape, BF16),
                pltpu.VMEM((1, HD), F32),
                pltpu.VMEM((1, HD), F32),
                pltpu.VMEM((nx, rows, HD), BF16),
                pltpu.VMEM((nx, rows, HD), BF16),
                pltpu.VMEM((rows, HD), BF16),
                pltpu.VMEM((nz, rows, HD), BF16),
                pltpu.VMEM((2, ny, nx, rows, HD), BF16),
                pltpu.VMEM((2 * ny, 9, 16, BLOCK), BF16),
                pltpu.VMEM((ny, BLOCK, HD), BF16),
                dma((10,)),
                dma((nx,)),
                dma((nx,)),
                dma((nz,)),
                dma((nz,)),
                dma((ny,)),
                dma((ny,)),
                dma((ny, nx)),
                dma((ny, nx)),
                dma((ny,)),
                dma((ny,)),
                dma((ny,)),
                dma((ny,)),
                dma((ny,)),
                dma((ny,)),
            ],
            compiler_params=pltpu.CompilerParams(
                collective_id=0, has_side_effects=True, vmem_limit_bytes=60 * 1024 * 1024
            ),
            name="encode_move_attend",
        )(
            clip_shape,
            packing,
            clip_features.reshape(FC * FRAME, features),
            conv_weight.reshape(-1, features),
            embed_weight,
            mod_scale.reshape(1, -1),
            mod_shift.reshape(1, -1),
            qkv_weight,
            q_gain.reshape(1, -1),
            k_gain.reshape(1, -1),
        )
        return out[None]

    return jax.shard_map(
        on_device,
        mesh=mesh,
        in_specs=(
            P("enc", "seq", None, None, None, None),
            P("enc", "seq", None),
            P("enc", "seq", None, None),
            P(),
            P(),
            P(),
            P(),
            P(None, "seq", "enc"),
            P(),
            P(),
        ),
        out_specs=P("seq", "enc", None),
        check_vma=False,
    )
```

```python
import functools
import math

import jax
import jax.numpy as jnp
from jax import lax
from jax.experimental import pallas as pl
from jax.experimental.pallas import tpu as pltpu
from jax.sharding import PartitionSpec as P

MESH = pl.DeviceIdType.MESH
F32 = jnp.float32
BF16 = jnp.bfloat16
EPS = 1e-06
LATF = 64
LAT = 16
TOK = 256
BLOCK = 128
FRAME = 256
FC = 4
HD = 128


def mod(a, n):
    return lax.rem(a, n)


def near_first(n):
    order = []
    for d in range(1, n // 2 + 1):
        order.append(d)
        if n - d != d:
            order.append(n - d)
    return order


def split_bf16(value, terms):
    parts = []
    for _ in range(terms):
        part = value.astype(BF16)
        parts.append(part)
        value = value - part.astype(F32)
    return parts


def nt_dot(a, b):
    return lax.dot_general(a, b, (((1,), (1,)), ((), ())), preferred_element_type=F32)


def partial_fold(s, embed_ref, scale_ref, shift_ref, w_ref):
    embed = embed_ref[...].astype(F32)
    mean = jnp.mean(embed, -1, keepdims=True)
    window = pl.ds(pl.multiple_of((s // 2) * 128, 128), 128)
    a_part = (embed_ref[:, window].astype(F32) - mean) * (1.0 + scale_ref[:, window])
    shift_rows = jnp.broadcast_to(shift_ref[:, window], (16, 128))
    lhs = jnp.concatenate([a_part, shift_rows], 0)
    hi, lo = split_bf16(lhs, 2)
    lhs2 = jnp.concatenate([hi, lo], 1)
    half = lax.broadcasted_iota(jnp.int32, (128, 3 * HD), 0) // 64
    w_all = jnp.concatenate([w_ref[0], w_ref[1], w_ref[2]], 1).astype(F32)
    w_two = jnp.concatenate([w_all, w_all], 0)
    w_pad = jnp.where(half == mod(s, 2), w_two, 0.0).astype(BF16)
    rhs = jnp.concatenate([w_pad, w_pad], 0)
    return jnp.dot(lhs2, rhs, preferred_element_type=F32)


def token_places(frames, height, width):
    slot = lax.broadcasted_iota(jnp.int32, (1, TOK), 1).astype(F32)
    zero = jnp.zeros((1, TOK), jnp.int32)
    frames_v = (zero + frames).astype(F32)
    half_h = (zero + height).astype(F32) * 0.5
    half_w = (zero + width).astype(F32) * 0.5
    per_frame = half_h * half_w
    t = jnp.floor((slot + 0.5) / per_frame)
    within = slot - t * per_frame
    r = jnp.floor((within + 0.5) / half_w)
    q = within - r * half_w
    count = frames_v * per_frame
    return jnp.where(slot < count, t * FRAME + r * 32.0 + q * 2.0, -1.0), count


def clip_frames(first, last, state, frames, height, width, feat_ref, conv_ref):
    products, tokens = state
    lane = lax.broadcasted_iota(jnp.int32, (1, FRAME), 1)
    row, col = lane // 16, lane % 16
    inside = (row < height) & (col < width)
    conv = conv_ref[...]
    places, _ = token_places(frames, height, width)
    spot = lax.broadcasted_iota(jnp.int32, (FRAME, TOK), 0).astype(F32)
    taps = 9 * LAT
    for t in range(first, last):
        here = nt_dot(conv, feat_ref[t * FRAME : (t + 1) * FRAME, :])
        keep = inside & (lane < jnp.where(t < frames, FRAME, 0))
        products.append(jnp.where(keep, here, 0.0))
        summed = products[t][2 * taps :]
        if t >= 1:
            summed = summed + products[t - 1][taps : 2 * taps]
        if t >= 2:
            summed = summed + products[t - 2][:taps]
        third = 3 * LAT
        rows = summed[third : 2 * third]
        rows = rows + jnp.where(row >= 1, pltpu.roll(summed[:third], 16, 1), 0.0)
        rows = rows + jnp.where(row <= 14, pltpu.roll(summed[2 * third :], FRAME - 16, 1), 0.0)
        latent = rows[LAT : 2 * LAT]
        latent = latent + jnp.where(col >= 1, pltpu.roll(rows[:LAT], 1, 1), 0.0)
        latent = latent + jnp.where(col <= 14, pltpu.roll(rows[2 * LAT :], FRAME - 1, 1), 0.0)
        latent = latent.astype(BF16).astype(F32)
        phases = [latent] + [pltpu.roll(latent, FRAME - d, 1) for d in (1, 16, 17)]
        phases = jnp.concatenate(phases, 0).astype(BF16)
        pick = jnp.where(spot + float(t * FRAME) == places, 1.0, 0.0).astype(BF16)
        tokens = tokens + jnp.dot(phases, pick, preferred_element_type=F32)
    return products, tokens


def in_feature_order(tokens):
    out_row = lax.broadcasted_iota(jnp.int32, (LATF, LATF), 0)
    in_row = lax.broadcasted_iota(jnp.int32, (LATF, LATF), 1)
    swap = jnp.where(in_row == (out_row % 4) * LAT + out_row // 4, 1.0, 0.0).astype(BF16)
    return jnp.dot(swap, tokens.astype(BF16), preferred_element_type=F32).astype(BF16)


def gram_terms(embed_ref):
    embed = embed_ref[...]
    features = embed.shape[1]
    both = nt_dot(embed, embed)
    wide = embed.astype(F32)
    mean_col = jnp.mean(wide, -1, keepdims=True)
    ones = jnp.ones((8, features), BF16)
    mean_row = nt_dot(ones, embed)[:1] * (1.0 / features)
    gram = both * (1.0 / features) - mean_col * mean_row
    return jnp.concatenate(split_bf16(gram, 3), 0)


def resplit(tile):
    row = lax.broadcasted_iota(jnp.int32, tile.shape, 0)
    total = tile + pltpu.roll(tile, tile.shape[0] - 3, 0)
    high = total.astype(BF16).astype(F32)
    low = pltpu.roll(total - high, 3, 0)
    return jnp.where(row < 3, high, jnp.where(row < 6, low, 0.0))


def pick_clip(e, count, x_all, gram):
    chosen = jnp.zeros((2, 4, 16, BLOCK), F32)
    is1 = jnp.zeros((1, BLOCK), F32)
    live = jnp.zeros((1, BLOCK), F32)
    me = (jnp.zeros((1, BLOCK), jnp.int32) + e).astype(F32)
    for j in range(count):
        info = x_all[j, 8].astype(F32)
        here1 = jnp.where(info[1:2] == me, 1.0, 0.0)
        here = jnp.where(info[0:1] == me, 1.0, 0.0) + here1
        is1 = is1 + here1
        live = live + here * info[2:3]
        chosen = chosen + x_all[j, 0:8].astype(F32).reshape(2, 4, 16, BLOCK) * here
    chosen = chosen.reshape(2, LATF, BLOCK)
    xt = jnp.concatenate([chosen[0].T, chosen[1].T], 0)
    xt16 = xt.astype(BF16)
    mixed = jnp.dot(jnp.concatenate([xt16, xt16, xt16], 1), gram, preferred_element_type=F32)
    var = jnp.sum(mixed * xt, -1, keepdims=True)
    scaled = xt * lax.rsqrt(jnp.maximum(var, 0.0) + EPS)
    high, low = split_bf16(scaled, 2)
    keys = jnp.concatenate([high, low], 1)
    rows = jnp.where(is1 > 0.5, keys[BLOCK:].astype(F32), keys[:BLOCK].astype(F32)).astype(BF16)
    q_slot = lax.broadcasted_iota(jnp.int32, (BLOCK, BLOCK), 0).astype(F32) + is1 * BLOCK
    q_live = jnp.where(q_slot < live, 1.0, 0.0)
    same = []
    for b in range(2):
        k_slot = lax.broadcasted_iota(jnp.int32, (1, BLOCK), 1).astype(F32) + float(b * BLOCK)
        k_live = jnp.where(k_slot < live, 1.0, 0.0)
        same.append(jnp.where(q_live == k_live, 1.0, 0.0))
    return keys, rows, jnp.concatenate(same, 1)


def project_head(keys, rows, fold, tail, gain):
    tail = tail.astype(F32)
    bias = tail[0:3] + tail[3:6]
    q_fold = jnp.concatenate([fold[0], fold[0]], 0)
    kv_fold = jnp.concatenate(fold[1:], 1)
    q = jnp.dot(rows, q_fold, preferred_element_type=F32) + bias[0:1]
    kv = jnp.dot(keys, jnp.concatenate([kv_fold, kv_fold], 0), preferred_element_type=F32)
    k = kv[:, :HD] + bias[1:2]
    q = q * lax.rsqrt(jnp.sum(q * q, -1, keepdims=True) + HD * EPS) * gain
    k = k * lax.rsqrt(jnp.sum(k * k, -1, keepdims=True) + HD * EPS)
    return q.astype(BF16), k.astype(BF16), kv[:, HD:].astype(BF16), bias[2:3]


def mix_head(q, k, v, v_bias, same):
    weights = (jnp.exp2(nt_dot(q, k)) * same).astype(BF16)
    ones = jnp.ones((TOK, HD), BF16)
    mixed = jnp.dot(weights, jnp.concatenate([v, ones], 1), preferred_element_type=F32)
    return (mixed[:, :HD] / mixed[:, HD:] + v_bias).astype(BF16)


def whole_kernel(
    ny,
    nz,
    nx,
    dims_hbm,
    plan_hbm,
    feat_hbm,
    conv_hbm,
    embed_hbm,
    scale_hbm,
    shift_hbm,
    w_hbm,
    qg_hbm,
    kg_hbm,
    out_ref,
    dims_ref,
    plan_ref,
    feat_ref,
    conv_ref,
    embed_ref,
    scale_ref,
    shift_ref,
    w_ref,
    qg_ref,
    kg_ref,
    stage,
    x_in,
    z_own,
    z_in,
    folds,
    x_all,
    crossing,
    in_sem,
    sendx,
    recvx,
    sendz,
    recvz,
    sendy,
    recvy,
    sendq,
    recvq,
    sendo,
    recvo,
    sendt,
    recvt,
    sendu,
    recvu,
):
    e = lax.axis_index("enc")
    s = lax.axis_index("seq")
    y, c = e // 2, mod(e, 2)
    z, x = s // nx, mod(s, nx)
    part_rows = LATF // nx
    fold_rows = 3 * part_rows

    def at_y(d):
        return {"enc": mod(y + d, ny) * 2 + c, "seq": s}

    def at_z(d):
        return {"enc": e, "seq": mod(z + d, nz) * nx + x}

    def at_x(d):
        return {"enc": e, "seq": z * nx + mod(x + d, nx)}

    sibling = {"enc": y * 2 + 1 - c, "seq": s}

    barrier = pltpu.get_barrier_semaphore()
    peers = [at_z(d) for d in reversed(near_first(nz))] + [at_y(d) for d in reversed(near_first(ny))]
    peers += [at_x(d) for d in reversed(near_first(nx))] + [sibling]
    for peer in peers:
        pl.semaphore_signal(barrier, inc=1, device_id=peer, device_id_type=MESH)

    loads = {}
    for i, (name, src, dst) in enumerate(
        [
            ("embed", embed_hbm, embed_ref),
            ("w", w_hbm, w_ref),
            ("scale", scale_hbm, scale_ref),
            ("shift", shift_hbm, shift_ref),
            ("dims", dims_hbm, dims_ref),
            ("plan", plan_hbm, plan_ref),
            ("conv", conv_hbm, conv_ref),
            ("feat", feat_hbm, feat_ref),
            ("qg", qg_hbm, qg_ref),
            ("kg", kg_hbm, kg_ref),
        ]
    ):
        loads[name] = pltpu.make_async_copy(src, dst, in_sem.at[i])
        loads[name].start()

    def settle(copies):
        for copy in copies:
            copy.wait_send()

    def send(src, dst, send_sem, recv_sem, peer):
        copy = pltpu.make_async_remote_copy(
            src_ref=src,
            dst_ref=dst,
            send_sem=send_sem,
            recv_sem=recv_sem,
            device_id=peer,
            device_id_type=MESH,
        )
        copy.start()
        return copy

    for name in ("embed", "w", "scale", "shift"):
        loads[name].wait()
    part = partial_fold(s, embed_ref, scale_ref, shift_ref, w_ref)
    row16 = lax.broadcasted_iota(jnp.int32, (16, HD), 0)
    bias = jnp.zeros((16, HD), F32)
    for j in range(3):
        bias = jnp.where(row16 == j, part[LATF : LATF + 16, j * HD : (j + 1) * HD], bias)
    bias = resplit(bias).astype(BF16)
    for g in range(nx):
        for j in range(3):
            stage[g, j * part_rows : (j + 1) * part_rows, :] = part[
                g * part_rows : (g + 1) * part_rows, j * HD : (j + 1) * HD
            ].astype(BF16)
        stage[g, fold_rows:, :] = bias

    for name in ("dims", "conv", "feat"):
        loads[name].wait()
    clip = (dims_ref[0, 0, 0], dims_ref[0, 0, 1], dims_ref[0, 0, 2])
    state = ([], jnp.zeros((LATF, TOK), F32))
    state = clip_frames(0, FC // 2, state, *clip, feat_ref, conv_ref)

    pl.semaphore_wait(barrier, len(peers))

    over_x = [
        send(stage.at[mod(x + d, nx)], x_in.at[d], sendx.at[d], recvx.at[d], at_x(d))
        for d in reversed(near_first(nx))
    ]

    state = clip_frames(FC // 2, FC, state, *clip, feat_ref, conv_ref)
    tokens = in_feature_order(state[1])
    _, count = token_places(*clip)
    loads["plan"].wait()
    for b in range(2):
        for i in range(4):
            x_all[e, 4 * b + i] = tokens[16 * i : 16 * i + 16, b * BLOCK : (b + 1) * BLOCK]
    owner0 = (jnp.zeros((16, BLOCK), jnp.int32) + plan_ref[0, 0, 0, 0]).astype(F32)
    owner1 = (jnp.zeros((16, BLOCK), jnp.int32) + plan_ref[0, 0, 1, 0]).astype(F32)
    meta = jnp.where(row16 == 0, owner0, jnp.where(row16 == 1, owner1, count[:, :BLOCK]))
    x_all[e, 8] = meta.astype(BF16)
    x_first = [
        send(x_all.at[e], x_all.at[e], sendt.at[d], recvt.at[d], at_y(d)) for d in near_first(ny)
    ]
    x_second = [send(x_all.at[e], x_all.at[e], sendu.at[0], recvu.at[0], sibling)]

    def finish(total):
        return jnp.concatenate([total[:fold_rows], resplit(total[fold_rows:])], 0).astype(BF16)

    total = stage[x].astype(F32)
    for copy in over_x:
        copy.wait_recv()
    for d in range(1, nx):
        total = total + x_in[d].astype(F32)
    z_own[...] = finish(total)
    over_z = [
        send(z_own, z_in.at[d], sendz.at[d], recvz.at[d], at_z(d))
        for d in reversed(near_first(nz))
    ]
    gram = gram_terms(embed_ref)

    def pass_tokens(d, copy):
        copy.wait_recv()
        source = mod(y - d + ny, ny) * 2 + c
        x_second.append(
            send(x_all.at[source], x_all.at[source], sendu.at[d], recvu.at[d], sibling)
        )

    arriving = list(zip(near_first(ny), x_first))
    early = len(arriving) // 2
    for d, copy in arriving[:early]:
        pass_tokens(d, copy)
    total = z_own[...].astype(F32)
    for copy in over_z:
        copy.wait_recv()
    for d in range(1, nz):
        total = total + z_in[d].astype(F32)
    folds[c, y, x] = finish(total)

    over_y = {}
    for d in ([1, 7, 2, 6, 4, 3, 5] if ny == 8 else near_first(ny)):
        mine = folds.at[c, y, x]
        over_y[d] = send(mine, mine, sendy.at[d], recvy.at[d], at_y(d))
    quarters = {}

    def source_y(d):
        return mod(y - d + ny, ny)

    def spread(d):
        if d:
            over_y[d].wait_recv()
        piece = folds.at[c, source_y(d), x, pl.ds(0, fold_rows)]
        quarters[d] = [
            send(piece, piece, sendq.at[d, dx], recvq.at[d, dx], at_x(dx))
            for dx in reversed(near_first(nx))
        ]

    def arrived(d):
        for copy in quarters[d]:
            copy.wait_recv()

    crossed = []
    order = [0] + near_first(ny)
    spread(order[0])
    for d, copy in arriving[early:]:
        pass_tokens(d, copy)
    for d in order[1:]:
        spread(d)
    settle(over_x + over_z + list(over_y.values()) + x_first)
    for copy in x_second:
        copy.wait_recv()
    settle(x_second)
    inputs = [pick_clip(owner, 2 * ny, x_all, gram) for owner in (2 * y + 1 - c, e)]
    for name in ("qg", "kg"):
        loads[name].wait()
    gain = qg_ref[...] * kg_ref[...] * (HD**0.5 * math.log2(math.e))

    def project(heads):
        projected = []
        for d, own in heads:
            keys, rows, _ = inputs[own]
            fold = [
                folds[c, source_y(d), :, j * part_rows : (j + 1) * part_rows, :].reshape(LATF, HD)
                for j in range(3)
            ]
            tail = folds[c, source_y(d), x, fold_rows:, :]
            projected.append(project_head(keys, rows, fold, tail, gain))
        return projected

    def mix(heads, projected):
        results = [
            mix_head(*parts, inputs[own][2]) for (d, own), parts in zip(heads, projected)
        ]
        for (d, own), result in zip(heads, results):
            column = pl.ds(pl.multiple_of((2 * source_y(d) + c) * HD, HD), HD)
            if own:
                out_ref[:, column] = result
            else:
                crossing[d] = result
                target = out_ref.at[:, column]
                crossed.append(send(crossing.at[d], target, sendo.at[d], recvo.at[d], sibling))

    first_half, second_half = order[: ny // 2 + 1], order[ny // 2 + 1 :]
    first = [(d, own) for own in (0, 1) for d in first_half]
    second = [(d, own) for own in (0, 1) for d in second_half]
    for d in first_half:
        arrived(d)
    mix(first, project(first))
    for d in second_half:
        arrived(d)
    second_parts = project(second)
    count = len(second_half)
    mix(second[:count], second_parts[:count])
    for d in order:
        settle(quarters[d])
    mix(second[count:], second_parts[count:])
    for copy in crossed:
        copy.wait_recv()
    settle(crossed)


def whole(memory=pltpu.VMEM):
    return pl.BlockSpec(memory_space=memory)


def solution(mesh):
    ny = mesh.shape["enc"] // 2
    nx = 4 if mesh.shape["seq"] == 32 else 2
    nz = mesh.shape["seq"] // nx
    fold_rows = 3 * LATF // nx
    rows = fold_rows + 16
    dma = pltpu.SemaphoreType.DMA

    def on_device(
        clip_features,
        clip_shape,
        packing,
        conv_weight,
        embed_weight,
        mod_shift,
        mod_scale,
        qkv_weight,
        q_gain,
        k_gain,
    ):
        features = clip_features.shape[-1]
        width = embed_weight.shape[1]
        out = pl.pallas_call(
            functools.partial(whole_kernel, ny, nz, nx),
            out_shape=pltpu.VMEM((BLOCK, 2 * ny * HD), BF16),
            in_specs=[whole(pltpu.HBM)] * 10,
            out_specs=whole(),
            scratch_shapes=[
                pltpu.SMEM((1, 1, 3), jnp.int32),
                pltpu.SMEM((1, 1, 2, 2), jnp.int32),
                pltpu.VMEM((FC * FRAME, features), BF16),
                pltpu.VMEM((27 * LAT, features), BF16),
                pltpu.VMEM((LATF, width), BF16),
                pltpu.VMEM((1, width), F32),
                pltpu.VMEM((1, width), F32),
                pltpu.VMEM(qkv_weight.shape, BF16),
                pltpu.VMEM((1, HD), F32),
                pltpu.VMEM((1, HD), F32),
                pltpu.VMEM((nx, rows, HD), BF16),
                pltpu.VMEM((nx, rows, HD), BF16),
                pltpu.VMEM((rows, HD), BF16),
                pltpu.VMEM((nz, rows, HD), BF16),
                pltpu.VMEM((2, ny, nx, rows, HD), BF16),
                pltpu.VMEM((2 * ny, 9, 16, BLOCK), BF16),
                pltpu.VMEM((ny, BLOCK, HD), BF16),
                dma((10,)),
                dma((nx,)),
                dma((nx,)),
                dma((nz,)),
                dma((nz,)),
                dma((ny,)),
                dma((ny,)),
                dma((ny, nx)),
                dma((ny, nx)),
                dma((ny,)),
                dma((ny,)),
                dma((ny,)),
                dma((ny,)),
                dma((ny,)),
                dma((ny,)),
            ],
            compiler_params=pltpu.CompilerParams(
                collective_id=0, has_side_effects=True, vmem_limit_bytes=60 * 1024 * 1024
            ),
            name="encode_move_attend",
        )(
            clip_shape,
            packing,
            clip_features.reshape(FC * FRAME, features),
            conv_weight.reshape(-1, features),
            embed_weight,
            mod_scale.reshape(1, -1),
            mod_shift.reshape(1, -1),
            qkv_weight,
            q_gain.reshape(1, -1),
            k_gain.reshape(1, -1),
        )
        return out[None]

    return jax.shard_map(
        on_device,
        mesh=mesh,
        in_specs=(
            P("enc", "seq", None, None, None, None),
            P("enc", "seq", None),
            P("enc", "seq", None, None),
            P(),
            P(),
            P(),
            P(),
            P(None, "seq", "enc"),
            P(),
            P(),
        ),
        out_specs=P("seq", "enc", None),
        check_vma=False,
    )
```

```python
import functools
import math

import jax
import jax.numpy as jnp
from jax import lax
from jax.experimental import pallas as pl
from jax.experimental.pallas import tpu as pltpu
from jax.sharding import PartitionSpec as P

MESH = pl.DeviceIdType.MESH
F32 = jnp.float32
BF16 = jnp.bfloat16
EPS = 1e-06
LATF = 64
LAT = 16
TOK = 256
BLOCK = 128
FRAME = 256
FC = 4
HD = 128


def mod(a, n):
    return lax.rem(a, n)


def near_first(n):
    order = []
    for d in range(1, n // 2 + 1):
        order.append(d)
        if n - d != d:
            order.append(n - d)
    return order


def split_bf16(value, terms):
    parts = []
    for _ in range(terms):
        part = value.astype(BF16)
        parts.append(part)
        value = value - part.astype(F32)
    return parts


def nt_dot(a, b):
    return lax.dot_general(a, b, (((1,), (1,)), ((), ())), preferred_element_type=F32)


def partial_fold(s, embed_ref, scale_ref, shift_ref, w_ref):
    embed = embed_ref[...].astype(F32)
    mean = jnp.mean(embed, -1, keepdims=True)
    window = pl.ds(pl.multiple_of((s // 2) * 128, 128), 128)
    a_part = (embed_ref[:, window].astype(F32) - mean) * (1.0 + scale_ref[:, window])
    shift_rows = jnp.broadcast_to(shift_ref[:, window], (16, 128))
    lhs = jnp.concatenate([a_part, shift_rows], 0)
    hi, lo = split_bf16(lhs, 2)
    lhs2 = jnp.concatenate([hi, lo], 1)
    half = lax.broadcasted_iota(jnp.int32, (128, 3 * HD), 0) // 64
    w_all = jnp.concatenate([w_ref[0], w_ref[1], w_ref[2]], 1).astype(F32)
    w_two = jnp.concatenate([w_all, w_all], 0)
    w_pad = jnp.where(half == mod(s, 2), w_two, 0.0).astype(BF16)
    rhs = jnp.concatenate([w_pad, w_pad], 0)
    return jnp.dot(lhs2, rhs, preferred_element_type=F32)


def token_places(frames, height, width):
    slot = lax.broadcasted_iota(jnp.int32, (1, TOK), 1).astype(F32)
    zero = jnp.zeros((1, TOK), jnp.int32)
    frames_v = (zero + frames).astype(F32)
    half_h = (zero + height).astype(F32) * 0.5
    half_w = (zero + width).astype(F32) * 0.5
    per_frame = half_h * half_w
    t = jnp.floor((slot + 0.5) / per_frame)
    within = slot - t * per_frame
    r = jnp.floor((within + 0.5) / half_w)
    q = within - r * half_w
    count = frames_v * per_frame
    return jnp.where(slot < count, t * FRAME + r * 32.0 + q * 2.0, -1.0), count


def clip_frames(first, last, state, frames, height, width, feat_ref, conv_ref):
    products, tokens = state
    lane = lax.broadcasted_iota(jnp.int32, (1, FRAME), 1)
    row, col = lane // 16, lane % 16
    inside = (row < height) & (col < width)
    conv = conv_ref[...]
    places, _ = token_places(frames, height, width)
    spot = lax.broadcasted_iota(jnp.int32, (FRAME, TOK), 0).astype(F32)
    taps = 9 * LAT
    for t in range(first, last):
        here = nt_dot(conv, feat_ref[t * FRAME : (t + 1) * FRAME, :])
        keep = inside & (lane < jnp.where(t < frames, FRAME, 0))
        products.append(jnp.where(keep, here, 0.0))
        summed = products[t][2 * taps :]
        if t >= 1:
            summed = summed + products[t - 1][taps : 2 * taps]
        if t >= 2:
            summed = summed + products[t - 2][:taps]
        third = 3 * LAT
        rows = summed[third : 2 * third]
        rows = rows + jnp.where(row >= 1, pltpu.roll(summed[:third], 16, 1), 0.0)
        rows = rows + jnp.where(row <= 14, pltpu.roll(summed[2 * third :], FRAME - 16, 1), 0.0)
        latent = rows[LAT : 2 * LAT]
        latent = latent + jnp.where(col >= 1, pltpu.roll(rows[:LAT], 1, 1), 0.0)
        latent = latent + jnp.where(col <= 14, pltpu.roll(rows[2 * LAT :], FRAME - 1, 1), 0.0)
        latent = latent.astype(BF16).astype(F32)
        phases = [latent] + [pltpu.roll(latent, FRAME - d, 1) for d in (1, 16, 17)]
        phases = jnp.concatenate(phases, 0).astype(BF16)
        pick = jnp.where(spot + float(t * FRAME) == places, 1.0, 0.0).astype(BF16)
        tokens = tokens + jnp.dot(phases, pick, preferred_element_type=F32)
    return products, tokens


def in_feature_order(tokens):
    out_row = lax.broadcasted_iota(jnp.int32, (LATF, LATF), 0)
    in_row = lax.broadcasted_iota(jnp.int32, (LATF, LATF), 1)
    swap = jnp.where(in_row == (out_row % 4) * LAT + out_row // 4, 1.0, 0.0).astype(BF16)
    return jnp.dot(swap, tokens.astype(BF16), preferred_element_type=F32).astype(BF16)


def gram_terms(embed_ref):
    embed = embed_ref[...]
    features = embed.shape[1]
    both = nt_dot(embed, embed)
    wide = embed.astype(F32)
    mean_col = jnp.mean(wide, -1, keepdims=True)
    ones = jnp.ones((8, features), BF16)
    mean_row = nt_dot(ones, embed)[:1] * (1.0 / features)
    gram = both * (1.0 / features) - mean_col * mean_row
    return jnp.concatenate(split_bf16(gram, 3), 0)


def resplit(tile):
    row = lax.broadcasted_iota(jnp.int32, tile.shape, 0)
    total = tile + pltpu.roll(tile, tile.shape[0] - 3, 0)
    high = total.astype(BF16).astype(F32)
    low = pltpu.roll(total - high, 3, 0)
    return jnp.where(row < 3, high, jnp.where(row < 6, low, 0.0))


def pick_clip(e, count, x_all, gram):
    chosen = jnp.zeros((2, 4, 16, BLOCK), F32)
    is1 = jnp.zeros((1, BLOCK), F32)
    live = jnp.zeros((1, BLOCK), F32)
    me = (jnp.zeros((1, BLOCK), jnp.int32) + e).astype(F32)
    for j in range(count):
        info = x_all[j, 8].astype(F32)
        here1 = jnp.where(info[1:2] == me, 1.0, 0.0)
        here = jnp.where(info[0:1] == me, 1.0, 0.0) + here1
        is1 = is1 + here1
        live = live + here * info[2:3]
        chosen = chosen + x_all[j, 0:8].astype(F32).reshape(2, 4, 16, BLOCK) * here
    chosen = chosen.reshape(2, LATF, BLOCK)
    xt = jnp.concatenate([chosen[0].T, chosen[1].T], 0)
    xt16 = xt.astype(BF16)
    mixed = jnp.dot(jnp.concatenate([xt16, xt16, xt16], 1), gram, preferred_element_type=F32)
    var = jnp.sum(mixed * xt, -1, keepdims=True)
    scaled = xt * lax.rsqrt(jnp.maximum(var, 0.0) + EPS)
    high, low = split_bf16(scaled, 2)
    keys = jnp.concatenate([high, low], 1)
    rows = jnp.where(is1 > 0.5, keys[BLOCK:].astype(F32), keys[:BLOCK].astype(F32)).astype(BF16)
    q_slot = lax.broadcasted_iota(jnp.int32, (BLOCK, BLOCK), 0).astype(F32) + is1 * BLOCK
    q_live = jnp.where(q_slot < live, 1.0, 0.0)
    same = []
    for b in range(2):
        k_slot = lax.broadcasted_iota(jnp.int32, (1, BLOCK), 1).astype(F32) + float(b * BLOCK)
        k_live = jnp.where(k_slot < live, 1.0, 0.0)
        same.append(jnp.where(q_live == k_live, 1.0, 0.0))
    return keys, rows, jnp.concatenate(same, 1)


def project_head(keys, rows, fold, tail, gain):
    tail = tail.astype(F32)
    bias = tail[0:3] + tail[3:6]
    q_fold = jnp.concatenate([fold[0], fold[0]], 0)
    kv_fold = jnp.concatenate(fold[1:], 1)
    q = jnp.dot(rows, q_fold, preferred_element_type=F32) + bias[0:1]
    kv = jnp.dot(keys, jnp.concatenate([kv_fold, kv_fold], 0), preferred_element_type=F32)
    k = kv[:, :HD] + bias[1:2]
    q = q * lax.rsqrt(jnp.sum(q * q, -1, keepdims=True) + HD * EPS) * gain
    k = k * lax.rsqrt(jnp.sum(k * k, -1, keepdims=True) + HD * EPS)
    return q.astype(BF16), k.astype(BF16), kv[:, HD:].astype(BF16), bias[2:3]


def mix_head(q, k, v, v_bias, same):
    weights = (jnp.exp2(nt_dot(q, k)) * same).astype(BF16)
    ones = jnp.ones((TOK, HD), BF16)
    mixed = jnp.dot(weights, jnp.concatenate([v, ones], 1), preferred_element_type=F32)
    return (mixed[:, :HD] / mixed[:, HD:] + v_bias).astype(BF16)


def whole_kernel(
    ny,
    nz,
    nx,
    dims_hbm,
    plan_hbm,
    feat_hbm,
    conv_hbm,
    embed_hbm,
    scale_hbm,
    shift_hbm,
    w_hbm,
    qg_hbm,
    kg_hbm,
    out_ref,
    dims_ref,
    plan_ref,
    feat_ref,
    conv_ref,
    embed_ref,
    scale_ref,
    shift_ref,
    w_ref,
    qg_ref,
    kg_ref,
    stage,
    x_in,
    z_own,
    z_in,
    folds,
    x_all,
    crossing,
    in_sem,
    sendx,
    recvx,
    sendz,
    recvz,
    sendy,
    recvy,
    sendq,
    recvq,
    sendo,
    recvo,
    sendt,
    recvt,
    sendu,
    recvu,
):
    e = lax.axis_index("enc")
    s = lax.axis_index("seq")
    y, c = e // 2, mod(e, 2)
    z, x = s // nx, mod(s, nx)
    part_rows = LATF // nx
    fold_rows = 3 * part_rows

    def at_y(d):
        return {"enc": mod(y + d, ny) * 2 + c, "seq": s}

    def at_z(d):
        return {"enc": e, "seq": mod(z + d, nz) * nx + x}

    def at_x(d):
        return {"enc": e, "seq": z * nx + mod(x + d, nx)}

    sibling = {"enc": y * 2 + 1 - c, "seq": s}

    barrier = pltpu.get_barrier_semaphore()
    peers = [at_z(d) for d in reversed(near_first(nz))] + [at_y(d) for d in reversed(near_first(ny))]
    peers += [at_x(d) for d in reversed(near_first(nx))] + [sibling]
    for peer in peers:
        pl.semaphore_signal(barrier, inc=1, device_id=peer, device_id_type=MESH)

    loads = {}
    for i, (name, src, dst) in enumerate(
        [
            ("embed", embed_hbm, embed_ref),
            ("w", w_hbm, w_ref),
            ("scale", scale_hbm, scale_ref),
            ("shift", shift_hbm, shift_ref),
            ("dims", dims_hbm, dims_ref),
            ("plan", plan_hbm, plan_ref),
            ("conv", conv_hbm, conv_ref),
            ("feat", feat_hbm, feat_ref),
            ("qg", qg_hbm, qg_ref),
            ("kg", kg_hbm, kg_ref),
        ]
    ):
        loads[name] = pltpu.make_async_copy(src, dst, in_sem.at[i])
        loads[name].start()

    def settle(copies):
        for copy in copies:
            copy.wait_send()

    def send(src, dst, send_sem, recv_sem, peer):
        copy = pltpu.make_async_remote_copy(
            src_ref=src,
            dst_ref=dst,
            send_sem=send_sem,
            recv_sem=recv_sem,
            device_id=peer,
            device_id_type=MESH,
        )
        copy.start()
        return copy

    for name in ("embed", "w", "scale", "shift"):
        loads[name].wait()
    part = partial_fold(s, embed_ref, scale_ref, shift_ref, w_ref)
    row16 = lax.broadcasted_iota(jnp.int32, (16, HD), 0)
    bias = jnp.zeros((16, HD), F32)
    for j in range(3):
        bias = jnp.where(row16 == j, part[LATF : LATF + 16, j * HD : (j + 1) * HD], bias)
    bias = resplit(bias).astype(BF16)
    for g in range(nx):
        for j in range(3):
            stage[g, j * part_rows : (j + 1) * part_rows, :] = part[
                g * part_rows : (g + 1) * part_rows, j * HD : (j + 1) * HD
            ].astype(BF16)
        stage[g, fold_rows:, :] = bias

    for name in ("dims", "conv", "feat"):
        loads[name].wait()
    clip = (dims_ref[0, 0, 0], dims_ref[0, 0, 1], dims_ref[0, 0, 2])
    state = ([], jnp.zeros((LATF, TOK), F32))
    state = clip_frames(0, FC // 2, state, *clip, feat_ref, conv_ref)

    pl.semaphore_wait(barrier, len(peers))

    over_x = [
        send(stage.at[mod(x + d, nx)], x_in.at[d], sendx.at[d], recvx.at[d], at_x(d))
        for d in reversed(near_first(nx))
    ]

    state = clip_frames(FC // 2, FC, state, *clip, feat_ref, conv_ref)
    tokens = in_feature_order(state[1])
    _, count = token_places(*clip)
    loads["plan"].wait()
    for b in range(2):
        for i in range(4):
            x_all[e, 4 * b + i] = tokens[16 * i : 16 * i + 16, b * BLOCK : (b + 1) * BLOCK]
    owner0 = (jnp.zeros((16, BLOCK), jnp.int32) + plan_ref[0, 0, 0, 0]).astype(F32)
    owner1 = (jnp.zeros((16, BLOCK), jnp.int32) + plan_ref[0, 0, 1, 0]).astype(F32)
    meta = jnp.where(row16 == 0, owner0, jnp.where(row16 == 1, owner1, count[:, :BLOCK]))
    x_all[e, 8] = meta.astype(BF16)
    def send_tokens(source, distance, step):
        piece = x_all.at[source]
        return send(piece, piece, sendt.at[distance], recvt.at[distance], at_y(step))

    relay = ny == 8
    x_first = {
        d: send_tokens(e, d, d) for d in ((2, 6, 1, 7) if relay else near_first(ny))
    }
    x_second = [send(x_all.at[e], x_all.at[e], sendu.at[0], recvu.at[0], sibling)]

    def finish(total):
        return jnp.concatenate([total[:fold_rows], resplit(total[fold_rows:])], 0).astype(BF16)

    total = stage[x].astype(F32)
    for copy in over_x:
        copy.wait_recv()
    for d in range(1, nx):
        total = total + x_in[d].astype(F32)
    z_own[...] = finish(total)
    over_z = [
        send(z_own, z_in.at[d], sendz.at[d], recvz.at[d], at_z(d))
        for d in reversed(near_first(nz))
    ]
    gram = gram_terms(embed_ref)

    def pass_tokens(d):
        x_first[d].wait_recv()
        source = mod(y - d + ny, ny) * 2 + c
        if relay and d == 2:
            x_first[3] = send_tokens(source, 3, 1)
            x_first[4] = send_tokens(source, 4, 2)
        if relay and d == 6:
            x_first[5] = send_tokens(source, 5, 7)
        x_second.append(
            send(x_all.at[source], x_all.at[source], sendu.at[d], recvu.at[d], sibling)
        )

    for d in list(x_first):
        pass_tokens(d)
    total = z_own[...].astype(F32)
    for copy in over_z:
        copy.wait_recv()
    for d in range(1, nz):
        total = total + z_in[d].astype(F32)
    folds[c, y, x] = finish(total)

    over_y = {}
    for d in ([1, 7, 2, 6, 4, 3, 5] if ny == 8 else near_first(ny)):
        mine = folds.at[c, y, x]
        over_y[d] = send(mine, mine, sendy.at[d], recvy.at[d], at_y(d))
    quarters = {}

    def source_y(d):
        return mod(y - d + ny, ny)

    def spread(d):
        if d:
            over_y[d].wait_recv()
        piece = folds.at[c, source_y(d), x, pl.ds(0, fold_rows)]
        quarters[d] = [
            send(piece, piece, sendq.at[d, dx], recvq.at[d, dx], at_x(dx))
            for dx in reversed(near_first(nx))
        ]

    def arrived(d):
        for copy in quarters[d]:
            copy.wait_recv()

    crossed = []
    order = [0] + near_first(ny)
    spread(order[0])
    for d in list(x_first)[4:]:
        pass_tokens(d)
    for d in order[1:]:
        spread(d)
    settle(over_x + over_z + list(over_y.values()) + list(x_first.values()))
    for copy in x_second:
        copy.wait_recv()
    settle(x_second)
    inputs = [pick_clip(owner, 2 * ny, x_all, gram) for owner in (2 * y + 1 - c, e)]
    for name in ("qg", "kg"):
        loads[name].wait()
    gain = qg_ref[...] * kg_ref[...] * (HD**0.5 * math.log2(math.e))

    def project(heads):
        projected = []
        for d, own in heads:
            keys, rows, _ = inputs[own]
            fold = [
                folds[c, source_y(d), :, j * part_rows : (j + 1) * part_rows, :].reshape(LATF, HD)
                for j in range(3)
            ]
            tail = folds[c, source_y(d), x, fold_rows:, :]
            projected.append(project_head(keys, rows, fold, tail, gain))
        return projected

    def mix(heads, projected):
        results = [
            mix_head(*parts, inputs[own][2]) for (d, own), parts in zip(heads, projected)
        ]
        for (d, own), result in zip(heads, results):
            column = pl.ds(pl.multiple_of((2 * source_y(d) + c) * HD, HD), HD)
            if own:
                out_ref[:, column] = result
            else:
                crossing[d] = result
                target = out_ref.at[:, column]
                crossed.append(send(crossing.at[d], target, sendo.at[d], recvo.at[d], sibling))

    first_half, second_half = order[: ny // 2 + 1], order[ny // 2 + 1 :]
    first = [(d, own) for own in (0, 1) for d in first_half]
    second = [(d, own) for own in (0, 1) for d in second_half]
    for d in first_half:
        arrived(d)
    mix(first, project(first))
    for d in second_half:
        arrived(d)
    second_parts = project(second)
    count = len(second_half)
    mix(second[:count], second_parts[:count])
    for d in order:
        settle(quarters[d])
    mix(second[count:], second_parts[count:])
    for copy in crossed:
        copy.wait_recv()
    settle(crossed)


def whole(memory=pltpu.VMEM):
    return pl.BlockSpec(memory_space=memory)


def solution(mesh):
    ny = mesh.shape["enc"] // 2
    nx = 4 if mesh.shape["seq"] == 32 else 2
    nz = mesh.shape["seq"] // nx
    fold_rows = 3 * LATF // nx
    rows = fold_rows + 16
    dma = pltpu.SemaphoreType.DMA

    def on_device(
        clip_features,
        clip_shape,
        packing,
        conv_weight,
        embed_weight,
        mod_shift,
        mod_scale,
        qkv_weight,
        q_gain,
        k_gain,
    ):
        features = clip_features.shape[-1]
        width = embed_weight.shape[1]
        out = pl.pallas_call(
            functools.partial(whole_kernel, ny, nz, nx),
            out_shape=pltpu.VMEM((BLOCK, 2 * ny * HD), BF16),
            in_specs=[whole(pltpu.HBM)] * 10,
            out_specs=whole(),
            scratch_shapes=[
                pltpu.SMEM((1, 1, 3), jnp.int32),
                pltpu.SMEM((1, 1, 2, 2), jnp.int32),
                pltpu.VMEM((FC * FRAME, features), BF16),
                pltpu.VMEM((27 * LAT, features), BF16),
                pltpu.VMEM((LATF, width), BF16),
                pltpu.VMEM((1, width), F32),
                pltpu.VMEM((1, width), F32),
                pltpu.VMEM(qkv_weight.shape, BF16),
                pltpu.VMEM((1, HD), F32),
                pltpu.VMEM((1, HD), F32),
                pltpu.VMEM((nx, rows, HD), BF16),
                pltpu.VMEM((nx, rows, HD), BF16),
                pltpu.VMEM((rows, HD), BF16),
                pltpu.VMEM((nz, rows, HD), BF16),
                pltpu.VMEM((2, ny, nx, rows, HD), BF16),
                pltpu.VMEM((2 * ny, 9, 16, BLOCK), BF16),
                pltpu.VMEM((ny, BLOCK, HD), BF16),
                dma((10,)),
                dma((nx,)),
                dma((nx,)),
                dma((nz,)),
                dma((nz,)),
                dma((ny,)),
                dma((ny,)),
                dma((ny, nx)),
                dma((ny, nx)),
                dma((ny,)),
                dma((ny,)),
                dma((ny,)),
                dma((ny,)),
                dma((ny,)),
                dma((ny,)),
            ],
            compiler_params=pltpu.CompilerParams(
                collective_id=0, has_side_effects=True, vmem_limit_bytes=60 * 1024 * 1024
            ),
            name="encode_move_attend",
        )(
            clip_shape,
            packing,
            clip_features.reshape(FC * FRAME, features),
            conv_weight.reshape(-1, features),
            embed_weight,
            mod_scale.reshape(1, -1),
            mod_shift.reshape(1, -1),
            qkv_weight,
            q_gain.reshape(1, -1),
            k_gain.reshape(1, -1),
        )
        return out[None]

    return jax.shard_map(
        on_device,
        mesh=mesh,
        in_specs=(
            P("enc", "seq", None, None, None, None),
            P("enc", "seq", None),
            P("enc", "seq", None, None),
            P(),
            P(),
            P(),
            P(),
            P(None, "seq", "enc"),
            P(),
            P(),
        ),
        out_specs=P("seq", "enc", None),
        check_vma=False,
    )
```
